32 devices in a mesh: pipe: 2 (over core), ctx: 16 (over z, y, x).
Axes of the slice: x: 2, y: 2, z: 4, core: 2. Of those that a mesh axis runs over, the one named last changes fastest.
Arguments:
- t_query: bfloat16 [2, 2048, 4096], P('pipe', 'ctx'), may hold values from -33 to 33
- t_key: bfloat16 [2, 2048, 512], P('pipe', 'ctx'), may hold values from -6 to 6
- t_value: bfloat16 [2, 2048, 512], P('pipe', 'ctx'), may hold values from -6 to 6
- s_query: bfloat16 [2, 2048, 4096], P('pipe', 'ctx'), may hold values from -33 to 33
- s_key: bfloat16 [2, 2048, 512], P('pipe', 'ctx'), may hold values from -6 to 6
- s_value: bfloat16 [2, 2048, 512], P('pipe', 'ctx'), may hold values from -6 to 6
- segment_ids: int32 [2048], replicated, may hold values from 0 to 15, never falling along the last dimension, each value on 1 to 256 neighbouring positions
Outputs:
- loss: float32 [], replicated
- query_grad: float32 [2, 2048, 4096], P('pipe', 'ctx')
- key_grad: float32 [2, 2048, 512], P('pipe', 'ctx')
- value_grad: float32 [2, 2048, 512], P('pipe', 'ctx')
The draws below stay inside these ranges and needn't reach their ends.
Inputs may be any that keep to these rules, and one draw needn't show every extreme that they name: `segment_ids`: segment ids never fall along the tokens; a document holds at most 256 tokens, and one holds exactly that many.
All inputs are finite; a program needn't handle non-finite values.
Results may differ from the reference program's by a relative error of at most 0.006.
Values may be sent and summed in bfloat16 or wider, within the bound.
A program may use at most 128 MiB of HBM per device.

```python
import math
import jax
import jax.numpy as jnp
import numpy as np
from jax import lax

TOK_DEV = 128
REACH = 2
HEADS = 32
KV_HEADS = 4
HEAD_DIM = 128
SECTIONS = 2
TOKENS = 2048


def drawn_pair(key, tag):
    base = jax.random.fold_in(key, tag)
    key_first, key_second = jax.random.split(base)
    group = HEADS // KV_HEADS
    shape_query = (SECTIONS, TOKENS, KV_HEADS, group, HEAD_DIM)
    shape_keys = (SECTIONS, TOKENS, KV_HEADS, HEAD_DIM)
    keys = jnp.clip(jax.random.normal(key_first, shape_keys, jnp.float32), -6.0, 6.0)
    query = jnp.clip(jax.random.normal(key_second, shape_query, jnp.float32), -6.0, 6.0)
    return (query.reshape(SECTIONS, TOKENS, HEADS * HEAD_DIM).astype(jnp.bfloat16), keys.reshape(SECTIONS, TOKENS, KV_HEADS * HEAD_DIM).astype(jnp.bfloat16))


def draw_t_query(key, part):
    return drawn_pair(key, 11)[0]


def draw_t_key(key, part):
    return drawn_pair(key, 11)[1]


def draw_s_query(key, part):
    return drawn_pair(key, 23)[0]


def draw_s_key(key, part):
    return drawn_pair(key, 23)[1]


def levels(own_key, dims, cuts, low, top_value):
    gain = 1.0
    for position, blocks in cuts:
        heights = jax.random.uniform(jax.random.fold_in(jax.random.fold_in(own_key, 6), position), (blocks,), jnp.float32, low / len(cuts), top_value / len(cuts))
        gain = gain * jnp.repeat(jnp.exp(heights), dims[position] // blocks).reshape((-1,) + (1,) * (len(dims) - 1 - position))
    return gain


def split_up(count, total, bound, lean):
    weights = [(1 << 20) // math.isqrt(grade ** lean) + 1 for grade in range(2, count + 1)]
    spare, given = total - bound - (count - 1), [1] * (count - 1)
    while spare > 0:
        free = [i for i in range(count - 1) if given[i] < bound]
        pool, left = sum([weights[i] for i in free]), spare
        for i in free:
            addition = min(bound - given[i], max(1, left * weights[i] // pool), spare)
            given[i] = given[i] + addition
            spare = spare - addition
    return np.array([bound] + given)


def ragged_sizes(stream_key, count, total, limit, slope):
    if count == 2:
        one = jax.random.randint(stream_key, (), max(1, total - limit), min(limit, total - 1) + 1)
        return jnp.stack([one, total - one])
    tallies = jnp.asarray(split_up(count, total, limit, slope), jnp.int32)
    pairs = (count - 1) // 2
    source_of, receiver = tallies[1:1 + 2 * pairs:2], tallies[2:2 + 2 * pairs:2]
    slack = jnp.minimum(source_of - 1, limit - receiver)
    passed = jax.random.randint(jax.random.fold_in(stream_key, 1), (pairs,), 0, 1 << 20) % (slack + 1)
    tallies = tallies.at[1:1 + 2 * pairs:2].set(source_of - passed).at[2:2 + 2 * pairs:2].set(receiver + passed)
    return tallies[jax.random.permutation(jax.random.fold_in(stream_key, 2), count)]


def scatter_about(rng, dims, width, bound, pieces=(), held_as=jnp.bfloat16):
    values = width * jax.random.normal(rng, dims, jnp.float32)
    if pieces:
        values = values * levels(rng, dims, pieces, -0.22, 0.18)
    return jnp.clip(values, -bound, bound).astype(held_as)


def setup_inputs(seed: int = 0) -> dict:
    streams_of = jax.random.split(jax.random.key(seed), 8)
    t_query = draw_t_query(jax.random.fold_in(streams_of[7], 71), 0)
    t_key = draw_t_key(jax.random.fold_in(streams_of[7], 71), 0)
    t_value = scatter_about(streams_of[2], (SECTIONS, TOKENS, KV_HEADS * HEAD_DIM), 1.0, 6.0, ((0, 2), (1, 16)))
    s_query = draw_s_query(jax.random.fold_in(streams_of[7], 71), 0)
    s_key = draw_s_key(jax.random.fold_in(streams_of[7], 71), 0)
    s_value = scatter_about(streams_of[5], (SECTIONS, TOKENS, KV_HEADS * HEAD_DIM), 1.0, 6.0, ((0, 2), (1, 16)))
    segment_ids = jnp.searchsorted(jnp.cumsum(ragged_sizes(streams_of[6], TOKENS // TOK_DEV, TOKENS, REACH * TOK_DEV, 1)), jnp.arange(TOKENS), side="right").astype(jnp.int32)
    return dict(t_query=t_query, t_key=t_key, t_value=t_value, s_query=s_query, s_key=s_key, s_value=s_value, segment_ids=segment_ids)


NEG_FILL = -1e+30

def attend(query_half, keys_half, values_half, allowed):
    tok_rows = query_half.shape[0]
    key_count = keys_half.shape[0]
    group = HEADS // KV_HEADS
    query_heads = query_half.reshape(tok_rows, KV_HEADS, group, HEAD_DIM).astype(jnp.float32)
    key_heads = keys_half.reshape(key_count, KV_HEADS, HEAD_DIM).astype(jnp.float32)
    value_heads = values_half.reshape(key_count, KV_HEADS, HEAD_DIM).astype(jnp.float32)
    scores = jnp.einsum('rkgd,wkd->kgrw', query_heads, key_heads) * HEAD_DIM ** (-0.5)
    scores = jnp.where(allowed[None, None], scores, NEG_FILL)
    row_peak = lax.optimization_barrier(jnp.max(scores, axis=-1, keepdims=True))
    expo = jnp.exp(scores - row_peak)
    row_total = lax.optimization_barrier(jnp.sum(expo, axis=-1, keepdims=True))
    weights = lax.optimization_barrier(expo.astype(jnp.bfloat16)).astype(jnp.float32)
    mixed = jnp.einsum('kgrw,wkd->rkgd', weights, value_heads) / jnp.transpose(row_total, (2, 0, 1, 3))
    return (mixed.reshape(tok_rows, HEADS * HEAD_DIM).astype(jnp.bfloat16), expo, row_total)

def attend_grad(query_half, keys_half, values_half, allowed, out_half, out_grad):
    tok_rows = query_half.shape[0]
    key_count = keys_half.shape[0]
    group = HEADS // KV_HEADS
    scale = HEAD_DIM ** (-0.5)
    unused_out, expo, row_total = attend(query_half, keys_half, values_half, allowed)
    query_heads = query_half.reshape(tok_rows, KV_HEADS, group, HEAD_DIM).astype(jnp.float32)
    key_heads = keys_half.reshape(key_count, KV_HEADS, HEAD_DIM).astype(jnp.float32)
    value_heads = values_half.reshape(key_count, KV_HEADS, HEAD_DIM).astype(jnp.float32)
    prob = expo / row_total
    prob_half = lax.optimization_barrier(prob.astype(jnp.bfloat16)).astype(jnp.float32)
    grad_half = lax.optimization_barrier(out_grad.astype(jnp.bfloat16)).astype(jnp.float32)
    grad_heads = grad_half.reshape(tok_rows, KV_HEADS, group, HEAD_DIM)
    out_heads = out_half.astype(jnp.float32).reshape(tok_rows, KV_HEADS, group, HEAD_DIM)
    value_win = jnp.einsum('kgrw,rkgd->wkd', prob_half, grad_heads)
    dprob = jnp.einsum('rkgd,wkd->kgrw', grad_heads, value_heads)
    delta = jnp.transpose(lax.optimization_barrier(jnp.sum(grad_heads * out_heads, axis=-1)), (1, 2, 0))
    dscore = prob * (dprob - delta[..., None])
    dscore = lax.optimization_barrier(dscore.astype(jnp.bfloat16)).astype(jnp.float32)
    query_grad = jnp.einsum('kgrw,wkd->rkgd', dscore, key_heads) * scale
    key_win = jnp.einsum('kgrw,rkgd->wkd', dscore, query_heads) * scale
    return (query_grad.reshape(tok_rows, HEADS * HEAD_DIM), key_win.reshape(key_count, KV_HEADS * HEAD_DIM), value_win.reshape(key_count, KV_HEADS * HEAD_DIM))

def reference(t_query, t_key, t_value, s_query, s_key, s_value, segment_ids):
    tok_rows = TOK_DEV
    key_pad = REACH * tok_rows
    key_span = key_pad + tok_rows
    key_width = KV_HEADS * HEAD_DIM
    seg_front = jnp.concatenate([jnp.full((key_pad,), -1, jnp.int32), segment_ids])
    causal = jnp.arange(key_span)[None, :] <= jnp.arange(tok_rows)[:, None] + key_pad
    starts = jnp.arange(TOKENS // tok_rows, dtype=jnp.int32) * tok_rows

    def allowed_at(start):
        key_seg = lax.dynamic_slice_in_dim(seg_front, start, key_span)
        query_seg = lax.dynamic_slice_in_dim(segment_ids, start, tok_rows)
        return (key_seg[None, :] == query_seg[:, None]) & causal

    def padded(keys):
        return jnp.concatenate([jnp.zeros((key_pad, key_width), keys.dtype), keys], axis=0)

    def section_forward(query, keys, values):
        keys_pad = padded(keys)
        values_pad = padded(values)

        def one_block(start):
            block_query = lax.dynamic_slice_in_dim(query, start, tok_rows)
            block_keys = lax.dynamic_slice_in_dim(keys_pad, start, key_span)
            block_values = lax.dynamic_slice_in_dim(values_pad, start, key_span)
            result, unused_expo, unused_total = attend(block_query, block_keys, block_values, allowed_at(start))
            return result
        return lax.map(one_block, starts).reshape(TOKENS, HEADS * HEAD_DIM)

    def section_backward(query, keys, values, out_half, out_grad):
        keys_pad = padded(keys)
        values_pad = padded(values)

        def one_block(carry, start):
            key_acc, value_acc = carry
            block_query = lax.dynamic_slice_in_dim(query, start, tok_rows)
            block_keys = lax.dynamic_slice_in_dim(keys_pad, start, key_span)
            block_values = lax.dynamic_slice_in_dim(values_pad, start, key_span)
            block_out = lax.dynamic_slice_in_dim(out_half, start, tok_rows)
            block_grad = lax.dynamic_slice_in_dim(out_grad, start, tok_rows)
            query_part, key_part, value_part = attend_grad(block_query, block_keys, block_values, allowed_at(start), block_out, block_grad)
            key_acc = lax.dynamic_update_slice_in_dim(key_acc, lax.dynamic_slice_in_dim(key_acc, start, key_span) + key_part, start, 0)
            value_acc = lax.dynamic_update_slice_in_dim(value_acc, lax.dynamic_slice_in_dim(value_acc, start, key_span) + value_part, start, 0)
            return ((key_acc, value_acc), query_part)
        empty = jnp.zeros((TOKENS + key_pad, key_width), jnp.float32)
        (key_acc, value_acc), query_parts = lax.scan(one_block, (empty, empty), starts)
        return (query_parts.reshape(TOKENS, HEADS * HEAD_DIM), key_acc[key_pad:], value_acc[key_pad:])
    teacher_outs = [section_forward(t_query[p], t_key[p], t_value[p]) for p in range(SECTIONS)]
    student_outs = [section_forward(s_query[p], s_key[p], s_value[p]) for p in range(SECTIONS)]
    zeros_full = jnp.zeros((TOKENS, HEADS * HEAD_DIM), jnp.float32)
    student_sum = zeros_full
    teacher_cum = zeros_full
    gaps = []
    for p in range(SECTIONS):
        student_sum = student_sum + student_outs[p].astype(jnp.float32)
        teacher_cum = teacher_cum + teacher_outs[p].astype(jnp.float32)
        if p + 1 < SECTIONS:
            ahead = teacher_outs[p + 1].astype(jnp.float32)
        else:
            ahead = zeros_full
        gaps.append(student_sum - (teacher_cum + ahead))
    squares = jnp.zeros((), jnp.float32)
    for p in range(SECTIONS):
        squares = squares + jnp.sum(gaps[p] * gaps[p])
    loss = squares / float(SECTIONS * TOKENS * HEADS * HEAD_DIM)
    running = zeros_full
    query_list = [None] * SECTIONS
    key_list = [None] * SECTIONS
    value_list = [None] * SECTIONS
    for p in reversed(range(SECTIONS)):
        running = running + gaps[p]
        query_list[p], key_list[p], value_list[p] = section_backward(s_query[p], s_key[p], s_value[p], student_outs[p], running)
    return (loss, jnp.stack(query_list), jnp.stack(key_list), jnp.stack(value_list))
```

```python
import functools
import math

import jax
import jax.numpy as jnp
from jax import lax
from jax.experimental import pallas as pl
from jax.experimental.pallas import tpu as pltpu
from jax.sharding import PartitionSpec as P

HEADS = 32
KV_HEADS = 4
HEAD_DIM = 128
GROUP = HEADS // KV_HEADS
WIDE = GROUP * HEAD_DIM
PAIR = 2 * HEAD_DIM
PAIRS = GROUP // 2
TEACHER, STUDENT = 0, 1
NEG_FILL = -1e30
MESH = pl.DeviceIdType.MESH
F32 = jnp.float32
BF16 = jnp.bfloat16


def dot(a, b):
    return jnp.dot(a, b, preferred_element_type=F32)


def dot_nt(a, b):
    return lax.dot_general(a, b, (((1,), (1,)), ((), ())), preferred_element_type=F32)


def loss_rounds(count):
    bits = count.bit_length() - 1
    return [list(range(low, min(low + 2, bits))) for low in range(0, bits, 2)]


def kernel(
    count, rows, denominator,
    tq, tk, tv, sq, sk, sv, seg,
    loss_out, qg_out, kg_out, vg_out,
    win, qbuf, bias, weights, outs, rinv, dnorm, delta, ex_tx, ex_rx, qgrad,
    own_grad, far_grad, txx, rxx, tx2, rx2, loss_acc, loss_buf,
    own_sem, q_sem, qg_sem, far_send, far_recv, near_send, near_recv,
    ex_send, ex_recv, gx_send, gx_recv, g2_send, g2_recv, loss_send, loss_recv,
):
    pipe = lax.axis_index("pipe")
    me = lax.axis_index("ctx")
    odd = lax.rem(me, 2)
    partner = me + 1 - 2 * odd
    has_prev = me >= 2
    has_next = me < count - 2
    span = 3 * rows
    scale = HEAD_DIM ** (-0.5)
    to_exp2 = scale * math.log2(math.e)
    rounds = loss_rounds(count)

    def xor(value, mask):
        result = value
        for bit in range(count.bit_length() - 1):
            if mask >> bit & 1:
                here = lax.rem(value // (1 << bit), 2)
                result = result + (1 << bit) * (1 - 2 * here)
        return result

    partners = []
    for number, bits in enumerate(rounds):
        masks = [sum(1 << b for k, b in enumerate(bits) if pick >> k & 1) for pick in range(1 << len(bits))]
        flips = (0, 1) if number == 0 else (0,)
        partners.append([(f, m) for f in flips for m in masks if f or m])

    def member(number):
        bits = rounds[number]
        place = lax.rem(me // (1 << bits[0]), 1 << len(bits))
        if number == 0:
            place = place + pipe * (1 << len(bits))
        return place

    def other(flip, mask):
        return (1 - pipe if flip else pipe, xor(me, mask))

    def own_copy(chunk, which):
        g, model = divmod(chunk, 2)
        source = ((tk, tv), (sk, sv))[model][which]
        return pltpu.make_async_copy(
            source.at[0, :, pl.ds(g * HEAD_DIM, HEAD_DIM)],
            win.at[chunk, which, pl.ds(2 * rows, rows), :],
            own_sem.at[chunk, which],
        )

    def q_copy(g, model):
        return pltpu.make_async_copy(
            (tq, sq)[model].at[0, :, pl.ds(g * WIDE, WIDE)], qbuf.at[model, g], q_sem.at[model, g]
        )

    for chunk in range(2 * KV_HEADS):
        for which in range(2):
            own_copy(chunk, which).start()
    for g in range(KV_HEADS):
        for model in (STUDENT, TEACHER):
            q_copy(g, model).start()

    barrier = pltpu.get_barrier_semaphore()
    greeted = 0
    for number in range(len(rounds)):
        for flip, mask in partners[number]:
            pl.semaphore_signal(barrier, inc=1, device_id=other(flip, mask), device_id_type=MESH)
            greeted += 1

    ahead = lax.rem(me // 2, 2)
    remaining = lax.rem(me - 2 + 4 * ahead + count, count)
    pl.semaphore_signal(barrier, inc=1, device_id=(pipe, remaining), device_id_type=MESH)
    greeted += 1

    query_seg = seg[pl.ds(me, 1), :]
    query_pos = lax.broadcasted_iota(jnp.int32, (rows, rows), 1)
    key_pos = lax.broadcasted_iota(jnp.int32, (rows, rows), 0)
    for slot in range(3):
        behind = 2 - slot
        source = jnp.maximum(me - behind, 0)
        key_seg = jnp.broadcast_to(seg[pl.ds(source, 1), :].astype(F32), (rows, rows)).T
        same = key_seg == query_seg.astype(F32)
        if behind == 0:
            same = same & (key_pos <= query_pos)
        fill = jnp.where(same, 0.0, NEG_FILL)
        if behind:
            fill = jnp.where(me >= behind, fill, NEG_FILL)
        bias[pl.ds(slot * rows, rows), :] = fill

    @pl.when(me < 2)
    def _():
        win[:, :, pl.ds(0, rows), :] = jnp.zeros((2 * KV_HEADS, 2, rows, HEAD_DIM), BF16)

    loss_acc[...] = jnp.zeros_like(loss_acc)
    pl.semaphore_wait(barrier, greeted)

    def far_copy(chunk):
        return pltpu.make_async_remote_copy(
            src_ref=win.at[chunk, :, pl.ds(2 * rows, rows), :],
            dst_ref=win.at[chunk, :, pl.ds(0, rows), :],
            send_sem=far_send.at[chunk],
            recv_sem=far_recv.at[chunk],
            device_id=(pipe, me + 2),
            device_id_type=MESH,
        )

    def near_copy(chunk, slot):
        return pltpu.make_async_remote_copy(
            src_ref=win.at[chunk, :, pl.ds(slot * rows, rows), :],
            dst_ref=win.at[chunk, :, pl.ds(rows, rows), :],
            send_sem=near_send.at[chunk],
            recv_sem=near_recv.at[chunk],
            device_id=(pipe, partner),
            device_id_type=MESH,
        )

    for g in range(KV_HEADS):
        for model in (STUDENT, TEACHER):
            chunk = 2 * g + model
            own_copy(chunk, 0).wait()
            own_copy(chunk, 1).wait()

            @pl.when(has_next)
            def _():
                far_copy(chunk).start()

            @pl.when(odd == 0)
            def _():
                near_copy(chunk, 2).start()

    def ex_copy(g):
        return pltpu.make_async_remote_copy(
            src_ref=ex_tx.at[g], dst_ref=ex_rx.at[g], send_sem=ex_send.at[g], recv_sem=ex_recv.at[g],
            device_id=(1 - pipe, me), device_id_type=MESH,
        )

    def gx_copy(g):
        return pltpu.make_async_remote_copy(
            src_ref=txx.at[g], dst_ref=rxx.at[g], send_sem=gx_send.at[g], recv_sem=gx_recv.at[g],
            device_id=(pipe, partner), device_id_type=MESH,
        )

    def g2_copy(g):
        return pltpu.make_async_remote_copy(
            src_ref=tx2.at[g], dst_ref=rx2.at[g], send_sem=g2_send.at[g], recv_sem=g2_recv.at[g],
            device_id=(pipe, me - 2), device_id_type=MESH,
        )

    def qg_copy(g):
        return pltpu.make_async_copy(
            qgrad.at[g], qg_out.at[0, :, pl.ds(pl.multiple_of(g * WIDE, WIDE), WIDE)], qg_sem.at[g]
        )

    def loss_copy(number, index):
        flip, mask = partners[number][index]
        mine = member(number)
        return pltpu.make_async_remote_copy(
            src_ref=loss_buf.at[number, mine],
            dst_ref=loss_buf.at[number, mine],
            send_sem=loss_send.at[number, index],
            recv_sem=loss_recv.at[number, index],
            device_id=other(flip, mask),
            device_id_type=MESH,
        )

    def loss_start(number, value):
        loss_buf[number, member(number)] = value
        for index in range(len(partners[number])):
            loss_copy(number, index).start()

    def loss_finish(number):
        for index in range(len(partners[number])):
            loss_copy(number, index).wait()
        total = loss_buf[number, 0]
        for place in range(1, len(partners[number]) + 1):
            total = total + loss_buf[number, place]
        return total

    pipe_f = pipe.astype(F32)
    odd_f = odd.astype(F32)

    def query_pair(model, g, hp):
        first = qbuf[model, g, :, pl.ds(hp * PAIR, HEAD_DIM)]
        second = qbuf[model, g, :, pl.ds(hp * PAIR + HEAD_DIM, HEAD_DIM)]
        return jnp.concatenate([first, second], axis=0)

    def forward(g):
        for model in (STUDENT, TEACHER):
            chunk = 2 * g + model

            @pl.when(has_prev)
            def _():
                far_copy(chunk).wait_recv()

            @pl.when(odd == 1)
            def _():
                near_copy(chunk, 0).start()

        slot = lax.rem(g, 2)
        for model in (STUDENT, TEACHER):
            chunk = 2 * g + model
            near_copy(chunk, 0).wait_recv()
            pltpu.make_async_copy(
                (tq, sq)[model].at[0, :, pl.ds(0, WIDE)], qbuf.at[model, g], q_sem.at[model, g]
            ).wait()
            keys = win[chunk, 0]
            values_t = win[chunk, 1].T
            for hp in range(PAIRS):
                cols = pl.ds(hp * PAIR, PAIR)
                fill = bias[...]
                scores = dot_nt(keys, query_pair(model, g, hp)) + jnp.concatenate([fill, fill], axis=1)
                peak = jnp.max(scores, axis=0, keepdims=True)
                expo = jnp.exp2((scores - peak) * to_exp2)
                inverse = 1.0 / jnp.sum(expo, axis=0, keepdims=True)
                half = expo.astype(BF16)
                if model == STUDENT:
                    weights[slot, :, cols] = half
                    rinv[g, :, cols] = inverse
                mixed = (dot(values_t, half) * inverse).astype(BF16)
                outs[model, g, :, cols] = mixed
                if model == TEACHER:
                    student = outs[STUDENT, g, :, cols].astype(F32)
                    ex_tx[g, :, cols] = (student - (1.0 + pipe_f) * mixed.astype(F32)).astype(BF16)
        ex_copy(g).start()

    def backward(g):
        slot = lax.rem(g, 2)
        chunk = 2 * g + STUDENT
        ex_copy(g).wait_recv()
        squares = jnp.zeros((8, PAIR), F32)
        for hp in range(PAIRS):
            cols = pl.ds(hp * PAIR, PAIR)
            student = outs[STUDENT, g, :, cols].astype(F32)
            teacher = outs[TEACHER, g, :, cols].astype(F32)
            taken = ex_rx[g, :, cols].astype(F32)
            apart = student - teacher
            first = taken - teacher
            second = taken + apart
            both = first * first + second * second
            squares = squares + jnp.sum(both.reshape(HEAD_DIM // 8, 8, PAIR), axis=0)
            grad = ((2.0 - pipe_f) * apart + taken) * rinv[g, :, cols]
            grad = grad.astype(BF16)
            dnorm[:, cols] = grad
            delta[:, cols] = jnp.sum(grad.astype(F32) * student, axis=0, keepdims=True)
        loss_acc[...] += pipe_f * (squares[:, :HEAD_DIM] + squares[:, HEAD_DIM:])

        @pl.when(g == KV_HEADS - 1)
        def _():
            loss_start(0, loss_acc[...])

        value_win = dot_nt(weights[slot], dnorm[...])
        keys_t = win[chunk, 0].T
        values = win[chunk, 1]
        key_win = jnp.zeros((span, HEAD_DIM), F32)
        for hp in range(PAIRS):
            cols = pl.ds(hp * PAIR, PAIR)
            dprob = dot(values, dnorm[:, cols])
            dscore = (weights[slot, :, cols].astype(F32) * (dprob - delta[:, cols])).astype(BF16)
            key_win = key_win + dot(dscore, query_pair(STUDENT, g, hp))
            query_t = dot(keys_t, dscore) * scale
            qgrad[g, :, pl.ds(hp * PAIR, HEAD_DIM)] = query_t[:, :HEAD_DIM].T
            qgrad[g, :, pl.ds(hp * PAIR + HEAD_DIM, HEAD_DIM)] = query_t[:, HEAD_DIM:].T
        qg_copy(g).start()
        key_win = key_win * scale
        for which, grads in enumerate((key_win, value_win)):
            far_grad[g, which] = grads[:rows]
            txx[g, which] = grads[rows : 2 * rows].astype(BF16)
            own_grad[g, which] = grads[2 * rows :]
        gx_copy(g).start()

    def pass_on(g):
        gx_copy(g).wait_recv()
        tx2[g] = (far_grad[g] + odd_f * rxx[g].astype(F32)).astype(BF16)

        @pl.when(has_prev)
        def _():
            g2_copy(g).start()

    def step(g, carry):
        @pl.when(g < KV_HEADS)
        def _():
            forward(g)

        @pl.when(g >= 1)
        def _():
            backward(g - 1)

        @pl.when(g >= 2)
        def _():
            pass_on(g - 2)

        return carry

    lax.fori_loop(0, KV_HEADS + 1, step, 0)
    pass_on(KV_HEADS - 1)

    @pl.when(me >= count - 2)
    def _():
        rx2[...] = jnp.zeros_like(rx2)

    for number in range(1, len(rounds)):
        loss_start(number, loss_finish(number - 1))
    for g in range(KV_HEADS):
        if g == KV_HEADS - 1:
            loss_out[0, 0] = jnp.sum(loss_finish(len(rounds) - 1)) / denominator

        @pl.when(has_next)
        def _():
            g2_copy(g).wait_recv()

        cols = pl.ds(g * HEAD_DIM, HEAD_DIM)
        for which, out in enumerate((kg_out, vg_out)):
            out[0, :, cols] = (
                own_grad[g, which] + rx2[g, which].astype(F32) + (1.0 - odd_f) * rxx[g, which].astype(F32)
            )

    for chunk in range(2 * KV_HEADS):
        near_copy(chunk, 0).wait_send()

        @pl.when(has_next)
        def _():
            far_copy(chunk).wait_send()

    for g in range(KV_HEADS):
        ex_copy(g).wait_send()
        gx_copy(g).wait_send()
        qg_copy(g).wait()

        @pl.when(has_prev)
        def _():
            g2_copy(g).wait_send()


def per_device(count, pipes, t_query, t_key, t_value, s_query, s_key, s_value, segment_ids):
    rows = t_query.shape[1]
    span = 3 * rows
    width = KV_HEADS * HEAD_DIM
    denominator = float(pipes * count * rows * HEADS * HEAD_DIM)
    rounds = len(loss_rounds(count))
    dma = pltpu.SemaphoreType.DMA
    anywhere = pl.BlockSpec(memory_space=pl.ANY)
    vmem = pl.BlockSpec(memory_space=pltpu.VMEM)
    loss, query_grad, key_grad, value_grad = pl.pallas_call(
        functools.partial(kernel, count, rows, denominator),
        out_shape=(
            jax.ShapeDtypeStruct((1, 1), F32),
            jax.ShapeDtypeStruct((1, rows, HEADS * HEAD_DIM), F32),
            jax.ShapeDtypeStruct((1, rows, width), F32),
            jax.ShapeDtypeStruct((1, rows, width), F32),
        ),
        in_specs=[anywhere] * 6 + [vmem],
        out_specs=(pl.BlockSpec(memory_space=pltpu.SMEM), anywhere, vmem, vmem),
        scratch_shapes=[
            pltpu.VMEM((2 * KV_HEADS, 2, span, HEAD_DIM), BF16),
            pltpu.VMEM((2, KV_HEADS, rows, WIDE), BF16),
            pltpu.VMEM((span, rows), F32),
            pltpu.VMEM((2, span, WIDE), BF16),
            pltpu.VMEM((2, KV_HEADS, HEAD_DIM, WIDE), BF16),
            pltpu.VMEM((KV_HEADS, 1, WIDE), F32),
            pltpu.VMEM((HEAD_DIM, WIDE), BF16),
            pltpu.VMEM((1, WIDE), F32),
            pltpu.VMEM((KV_HEADS, HEAD_DIM, WIDE), BF16),
            pltpu.VMEM((KV_HEADS, HEAD_DIM, WIDE), BF16),
            pltpu.VMEM((KV_HEADS, rows, WIDE), F32),
            pltpu.VMEM((KV_HEADS, 2, rows, HEAD_DIM), F32),
            pltpu.VMEM((KV_HEADS, 2, rows, HEAD_DIM), F32),
            pltpu.VMEM((KV_HEADS, 2, rows, HEAD_DIM), BF16),
            pltpu.VMEM((KV_HEADS, 2, rows, HEAD_DIM), BF16),
            pltpu.VMEM((KV_HEADS, 2, rows, HEAD_DIM), BF16),
            pltpu.VMEM((KV_HEADS, 2, rows, HEAD_DIM), BF16),
            pltpu.VMEM((8, HEAD_DIM), F32),
            pltpu.VMEM((rounds, 8, 8, HEAD_DIM), F32),
            dma((2 * KV_HEADS, 2)),
            dma((2, KV_HEADS)),
            dma((KV_HEADS,)),
            dma((2 * KV_HEADS,)),
            dma((2 * KV_HEADS,)),
            dma((2 * KV_HEADS,)),
            dma((2 * KV_HEADS,)),
            dma((KV_HEADS,)),
            dma((KV_HEADS,)),
            dma((KV_HEADS,)),
            dma((KV_HEADS,)),
            dma((KV_HEADS,)),
            dma((KV_HEADS,)),
            dma((rounds, 8)),
            dma((rounds, 8)),
        ],
        compiler_params=pltpu.CompilerParams(
            collective_id=0, has_side_effects=True, vmem_limit_bytes=40 * 1024 * 1024
        ),
        cost_estimate=pl.CostEstimate(
            flops=8 * 2 * HEADS * rows * span * HEAD_DIM,
            bytes_accessed=6 * 1024 * 1024,
            transcendentals=2 * HEADS * rows * span,
        ),
    )(t_query, t_key, t_value, s_query, s_key, s_value, segment_ids.reshape(count, rows))
    return loss.reshape(()), query_grad, key_grad, value_grad


def solution(mesh):
    spread = P("pipe", "ctx", None)
    return jax.shard_map(
        functools.partial(per_device, mesh.shape["ctx"], mesh.shape["pipe"]),
        mesh=mesh,
        in_specs=(spread,) * 6 + (P(),),
        out_specs=(P(), spread, spread, spread),
        check_vma=False,
    )
```

```python
import functools
import math

import jax
import jax.numpy as jnp
from jax import lax
from jax.experimental import pallas as pl
from jax.experimental.pallas import tpu as pltpu
from jax.sharding import PartitionSpec as P

HEADS = 32
KV_HEADS = 4
HEAD_DIM = 128
GROUP = HEADS // KV_HEADS
WIDE = GROUP * HEAD_DIM
PAIR = 2 * HEAD_DIM
PAIRS = GROUP // 2
TEACHER, STUDENT = 0, 1
NEG_FILL = -1e30
MESH = pl.DeviceIdType.MESH
F32 = jnp.float32
BF16 = jnp.bfloat16


def dot(a, b):
    return jnp.dot(a, b, preferred_element_type=F32)


def dot_nt(a, b):
    return lax.dot_general(a, b, (((1,), (1,)), ((), ())), preferred_element_type=F32)


def loss_rounds(count):
    bits = count.bit_length() - 1
    return [list(range(low, min(low + 2, bits))) for low in range(0, bits, 2)]


def kernel(
    count, rows, denominator,
    tq, tk, tv, sq, sk, sv, seg,
    loss_out, qg_out, kg_out, vg_out,
    win, qbuf, bias, weights, outs, rinv, dnorm, delta, dscore, ex_tx, ex_rx, qgrad,
    own_grad, far_grad, txx, rxx, tx2, rx2, loss_acc, loss_buf,
    own_sem, q_sem, qg_sem, far_send, far_recv, near_send, near_recv,
    ex_send, ex_recv, gx_send, gx_recv, g2_send, g2_recv, loss_send, loss_recv,
):
    pipe = lax.axis_index("pipe")
    me = lax.axis_index("ctx")
    odd = lax.rem(me, 2)
    partner = me + 1 - 2 * odd
    has_prev = me >= 2
    has_next = me < count - 2
    scale = HEAD_DIM ** (-0.5)
    to_exp2 = scale * math.log2(math.e)
    rounds = loss_rounds(count)

    def xor(value, mask):
        result = value
        for bit in range(count.bit_length() - 1):
            if mask >> bit & 1:
                here = lax.rem(value // (1 << bit), 2)
                result = result + (1 << bit) * (1 - 2 * here)
        return result

    partners = []
    for number, bits in enumerate(rounds):
        masks = [sum(1 << b for k, b in enumerate(bits) if pick >> k & 1) for pick in range(1 << len(bits))]
        flips = (0, 1) if number == 0 else (0,)
        partners.append([(f, m) for f in flips for m in masks if f or m])

    def member(number):
        bits = rounds[number]
        place = lax.rem(me // (1 << bits[0]), 1 << len(bits))
        if number == 0:
            place = place + pipe * (1 << len(bits))
        return place

    def other(flip, mask):
        return (1 - pipe if flip else pipe, xor(me, mask))

    def own_copy(chunk, which):
        g, model = divmod(chunk, 2)
        source = ((tk, tv), (sk, sv))[model][which]
        return pltpu.make_async_copy(
            source.at[0, :, pl.ds(g * HEAD_DIM, HEAD_DIM)],
            win.at[chunk, which, pl.ds(2 * rows, rows), :],
            own_sem.at[chunk, which],
        )

    def q_copy(g, model):
        return pltpu.make_async_copy(
            (tq, sq)[model].at[0, :, pl.ds(g * WIDE, WIDE)], qbuf.at[model, g], q_sem.at[model, g]
        )

    for chunk in range(2 * KV_HEADS):
        for which in range(2):
            own_copy(chunk, which).start()
    for g in range(KV_HEADS):
        for model in (STUDENT, TEACHER):
            q_copy(g, model).start()

    barrier = pltpu.get_barrier_semaphore()
    greeted = 0
    for number in range(len(rounds)):
        for flip, mask in partners[number]:
            pl.semaphore_signal(barrier, inc=1, device_id=other(flip, mask), device_id_type=MESH)
            greeted += 1

    ahead = lax.rem(me // 2, 2)
    remaining = lax.rem(me - 2 + 4 * ahead + count, count)
    pl.semaphore_signal(barrier, inc=1, device_id=(pipe, remaining), device_id_type=MESH)
    greeted += 1

    query_seg = seg[pl.ds(me, 1), :].astype(F32)
    query_pos = lax.broadcasted_iota(jnp.int32, (rows, rows), 1)
    key_pos = lax.broadcasted_iota(jnp.int32, (rows, rows), 0)

    def fill_of(behind):
        source = jnp.maximum(me - behind, 0)
        key_seg = jnp.broadcast_to(seg[pl.ds(source, 1), :].astype(F32), (rows, rows)).T
        fill = jnp.where(key_seg == query_seg, 0.0, NEG_FILL)
        return jnp.where(me >= behind, fill, NEG_FILL)

    bias[pl.ds(0, rows), :] = fill_of(1)
    bias[pl.ds(rows, rows), :] = jnp.where(key_pos <= query_pos, fill_of(0), fill_of(2))

    @pl.when(me < 2)
    def _():
        win[:, :, pl.ds(0, rows), :] = jnp.zeros((2 * KV_HEADS, 2, rows, HEAD_DIM), BF16)

    loss_acc[...] = jnp.zeros_like(loss_acc)
    pl.semaphore_wait(barrier, greeted)

    def far_copy(chunk):
        return pltpu.make_async_remote_copy(
            src_ref=win.at[chunk, :, pl.ds(2 * rows, rows), :],
            dst_ref=win.at[chunk, :, pl.ds(0, rows), :],
            send_sem=far_send.at[chunk],
            recv_sem=far_recv.at[chunk],
            device_id=(pipe, me + 2),
            device_id_type=MESH,
        )

    def near_copy(chunk, slot):
        return pltpu.make_async_remote_copy(
            src_ref=win.at[chunk, :, pl.ds(slot * rows, rows), :],
            dst_ref=win.at[chunk, :, pl.ds(rows, rows), :],
            send_sem=near_send.at[chunk],
            recv_sem=near_recv.at[chunk],
            device_id=(pipe, partner),
            device_id_type=MESH,
        )

    for g in range(KV_HEADS):
        for model in (STUDENT, TEACHER):
            chunk = 2 * g + model
            own_copy(chunk, 0).wait()
            own_copy(chunk, 1).wait()

            @pl.when(has_next)
            def _():
                far_copy(chunk).start()

            @pl.when(odd == 0)
            def _():
                near_copy(chunk, 2).start()

    def ex_copy(g):
        return pltpu.make_async_remote_copy(
            src_ref=ex_tx.at[g], dst_ref=ex_rx.at[g], send_sem=ex_send.at[g], recv_sem=ex_recv.at[g],
            device_id=(1 - pipe, me), device_id_type=MESH,
        )

    def gx_copy(g):
        return pltpu.make_async_remote_copy(
            src_ref=txx.at[g], dst_ref=rxx.at[g], send_sem=gx_send.at[g], recv_sem=gx_recv.at[g],
            device_id=(pipe, partner), device_id_type=MESH,
        )

    def g2_copy(g):
        return pltpu.make_async_remote_copy(
            src_ref=tx2.at[g], dst_ref=rx2.at[g], send_sem=g2_send.at[g], recv_sem=g2_recv.at[g],
            device_id=(pipe, me - 2), device_id_type=MESH,
        )

    def qg_copy(g):
        return pltpu.make_async_copy(
            qgrad.at[g], qg_out.at[0, :, pl.ds(pl.multiple_of(g * WIDE, WIDE), WIDE)], qg_sem.at[g]
        )

    def loss_copy(number, index):
        flip, mask = partners[number][index]
        mine = member(number)
        return pltpu.make_async_remote_copy(
            src_ref=loss_buf.at[number, mine],
            dst_ref=loss_buf.at[number, mine],
            send_sem=loss_send.at[number, index],
            recv_sem=loss_recv.at[number, index],
            device_id=other(flip, mask),
            device_id_type=MESH,
        )

    def loss_start(number, value):
        loss_buf[number, member(number)] = value
        for index in range(len(partners[number])):
            loss_copy(number, index).start()

    def loss_finish(number):
        for index in range(len(partners[number])):
            loss_copy(number, index).wait()
        total = loss_buf[number, 0]
        for place in range(1, len(partners[number]) + 1):
            total = total + loss_buf[number, place]
        return total

    pipe_f = pipe.astype(F32)
    odd_f = odd.astype(F32)

    def query_pair(model, g, hp):
        first = qbuf[model, g, :, pl.ds(hp * PAIR, HEAD_DIM)]
        second = qbuf[model, g, :, pl.ds(hp * PAIR + HEAD_DIM, HEAD_DIM)]
        return jnp.concatenate([first, second], axis=0)

    def wide_iota(axis):
        return lax.broadcasted_iota(jnp.int32, (rows, PAIR), axis)

    def forward(g):
        for model in (STUDENT, TEACHER):
            chunk = 2 * g + model

            @pl.when(has_prev)
            def _():
                far_copy(chunk).wait_recv()

            @pl.when(odd == 1)
            def _():
                near_copy(chunk, 0).start()

        for model in (STUDENT, TEACHER):
            near_copy(2 * g + model, 0).wait_recv()
            pltpu.make_async_copy(
                (tq, sq)[model].at[0, :, pl.ds(0, WIDE)], qbuf.at[model, g], q_sem.at[model, g]
            ).wait()

        slot = lax.rem(g, 2)
        triangle = wide_iota(0) <= lax.rem(wide_iota(1), rows)
        steps = [(model, hp) for model in (STUDENT, TEACHER) for hp in range(PAIRS)]

        def raw_scores(model, hp):
            return dot_nt(win[2 * g + model, 0], query_pair(model, g, hp))

        def finish(model, hp, mixed, inverse):
            cols = pl.ds(hp * PAIR, PAIR)
            mixed = (mixed * inverse).astype(BF16)
            outs[model, g, :, cols] = mixed
            if model == TEACHER:
                student = outs[STUDENT, g, :, cols].astype(F32)
                ex_tx[g, :, cols] = (student - (1.0 + pipe_f) * mixed.astype(F32)).astype(BF16)

        values_t = [win[2 * g + model, 1].T for model in (TEACHER, STUDENT)]
        later = raw_scores(*steps[0])
        pending = None
        for index, (model, hp) in enumerate(steps):
            cols = pl.ds(hp * PAIR, PAIR)
            raw = later
            if index + 1 < len(steps):
                later = raw_scores(*steps[index + 1])
            fill = bias[pl.ds(0, rows), :]
            middle = raw[rows : 2 * rows] + jnp.concatenate([fill, fill], axis=1)
            fill = bias[pl.ds(rows, rows), :]
            edge = jnp.where(triangle, raw[2 * rows :], raw[:rows]) + jnp.concatenate([fill, fill], axis=1)
            peak = jnp.max(jnp.maximum(middle, edge), axis=0, keepdims=True)
            middle = jnp.exp2((middle - peak) * to_exp2)
            edge = jnp.exp2((edge - peak) * to_exp2)
            inverse = 1.0 / jnp.sum(middle + edge, axis=0, keepdims=True)
            half = jnp.concatenate(
                [
                    jnp.where(triangle, 0.0, edge).astype(BF16),
                    middle.astype(BF16),
                    jnp.where(triangle, edge, 0.0).astype(BF16),
                ],
                axis=0,
            )
            if model == STUDENT:
                weights[slot, :, cols] = half
                rinv[g, :, cols] = inverse
            if pending is not None:
                finish(*pending)
            pending = (model, hp, dot(values_t[model], half), inverse)
        finish(*pending)
        ex_copy(g).start()

    def backward(g):
        slot = lax.rem(g, 2)
        chunk = 2 * g + STUDENT
        ex_copy(g).wait_recv()
        squares = jnp.zeros((8, PAIR), F32)
        for hp in range(PAIRS):
            cols = pl.ds(hp * PAIR, PAIR)
            student = outs[STUDENT, g, :, cols].astype(F32)
            teacher = outs[TEACHER, g, :, cols].astype(F32)
            taken = ex_rx[g, :, cols].astype(F32)
            apart = student - teacher
            first = taken - teacher
            second = taken + apart
            both = first * first + second * second
            squares = squares + jnp.sum(both.reshape(HEAD_DIM // 8, 8, PAIR), axis=0)
            grad = ((2.0 - pipe_f) * apart + taken) * rinv[g, :, cols]
            grad = grad.astype(BF16)
            dnorm[:, cols] = grad
            delta[:, cols] = jnp.sum(grad.astype(F32) * student, axis=0, keepdims=True)
        loss_acc[...] += pipe_f * (squares[:, :HEAD_DIM] + squares[:, HEAD_DIM:])

        @pl.when(g == KV_HEADS - 1)
        def _():
            loss_start(0, loss_acc[...])

        def dprob_of(hp):
            return dot(win[chunk, 1], dnorm[:, pl.ds(hp * PAIR, PAIR)])

        later = dprob_of(0)
        for hp in range(PAIRS):
            cols = pl.ds(hp * PAIR, PAIR)
            dprob = later
            if hp + 1 < PAIRS:
                later = dprob_of(hp + 1)
            else:
                value_win = dot_nt(weights[slot], dnorm[...])
            dscore[:, cols] = (weights[slot, :, cols].astype(F32) * (dprob - delta[:, cols])).astype(BF16)
        queries = jnp.concatenate(
            [qbuf[STUDENT, g, :, pl.ds(h * HEAD_DIM, HEAD_DIM)] for h in range(GROUP)], axis=0
        )
        key_win = dot(dscore[...], queries) * scale
        for which, grads in enumerate((key_win, value_win)):
            far_grad[g, which] = grads[:rows]
            txx[g, which] = grads[rows : 2 * rows].astype(BF16)
            own_grad[g, which] = grads[2 * rows :]
        gx_copy(g).start()
        keys_t = win[chunk, 0].T
        for hp in range(PAIRS):
            query_t = dot(keys_t, dscore[:, pl.ds(hp * PAIR, PAIR)]) * scale
            qgrad[g, :, pl.ds(hp * PAIR, HEAD_DIM)] = query_t[:, :HEAD_DIM].T
            qgrad[g, :, pl.ds(hp * PAIR + HEAD_DIM, HEAD_DIM)] = query_t[:, HEAD_DIM:].T
        qg_copy(g).start()

    def pass_on(g):
        gx_copy(g).wait_recv()
        tx2[g] = (far_grad[g] + odd_f * rxx[g].astype(F32)).astype(BF16)

        @pl.when(has_prev)
        def _():
            g2_copy(g).start()

    def step(g, carry):
        @pl.when(g < KV_HEADS)
        def _():
            forward(g)

        @pl.when(g >= 1)
        def _():
            backward(g - 1)

        @pl.when(g >= 2)
        def _():
            pass_on(g - 2)

        return carry

    lax.fori_loop(0, KV_HEADS + 1, step, 0)
    pass_on(KV_HEADS - 1)

    @pl.when(me >= count - 2)
    def _():
        rx2[...] = jnp.zeros_like(rx2)

    for number in range(1, len(rounds)):
        loss_start(number, loss_finish(number - 1))
    for g in range(KV_HEADS):
        if g == KV_HEADS - 1:
            loss_out[0, 0] = jnp.sum(loss_finish(len(rounds) - 1)) / denominator

        @pl.when(has_next)
        def _():
            g2_copy(g).wait_recv()

        cols = pl.ds(g * HEAD_DIM, HEAD_DIM)
        for which, out in enumerate((kg_out, vg_out)):
            out[0, :, cols] = (
                own_grad[g, which] + rx2[g, which].astype(F32) + (1.0 - odd_f) * rxx[g, which].astype(F32)
            )

    for chunk in range(2 * KV_HEADS):
        near_copy(chunk, 0).wait_send()

        @pl.when(has_next)
        def _():
            far_copy(chunk).wait_send()

    for g in range(KV_HEADS):
        ex_copy(g).wait_send()
        gx_copy(g).wait_send()
        qg_copy(g).wait()

        @pl.when(has_prev)
        def _():
            g2_copy(g).wait_send()


def per_device(count, pipes, t_query, t_key, t_value, s_query, s_key, s_value, segment_ids):
    rows = t_query.shape[1]
    span = 3 * rows
    width = KV_HEADS * HEAD_DIM
    denominator = float(pipes * count * rows * HEADS * HEAD_DIM)
    rounds = len(loss_rounds(count))
    dma = pltpu.SemaphoreType.DMA
    anywhere = pl.BlockSpec(memory_space=pltpu.HBM)
    vmem = pl.BlockSpec(memory_space=pltpu.VMEM)
    loss, query_grad, key_grad, value_grad = pl.pallas_call(
        functools.partial(kernel, count, rows, denominator),
        out_shape=(
            jax.ShapeDtypeStruct((1, 1), F32),
            jax.ShapeDtypeStruct((1, rows, HEADS * HEAD_DIM), F32),
            jax.ShapeDtypeStruct((1, rows, width), F32),
            jax.ShapeDtypeStruct((1, rows, width), F32),
        ),
        in_specs=[anywhere] * 6 + [vmem],
        out_specs=(pl.BlockSpec(memory_space=pltpu.SMEM), anywhere, vmem, vmem),
        scratch_shapes=[
            pltpu.VMEM((2 * KV_HEADS, 2, span, HEAD_DIM), BF16),
            pltpu.VMEM((2, KV_HEADS, rows, WIDE), BF16),
            pltpu.VMEM((2 * rows, rows), F32),
            pltpu.VMEM((2, span, WIDE), BF16),
            pltpu.VMEM((2, KV_HEADS, HEAD_DIM, WIDE), BF16),
            pltpu.VMEM((KV_HEADS, 1, WIDE), F32),
            pltpu.VMEM((HEAD_DIM, WIDE), BF16),
            pltpu.VMEM((1, WIDE), F32),
            pltpu.VMEM((span, WIDE), BF16),
            pltpu.VMEM((KV_HEADS, HEAD_DIM, WIDE), BF16),
            pltpu.VMEM((KV_HEADS, HEAD_DIM, WIDE), BF16),
            pltpu.VMEM((KV_HEADS, rows, WIDE), F32),
            pltpu.VMEM((KV_HEADS, 2, rows, HEAD_DIM), F32),
            pltpu.VMEM((KV_HEADS, 2, rows, HEAD_DIM), F32),
            pltpu.VMEM((KV_HEADS, 2, rows, HEAD_DIM), BF16),
            pltpu.VMEM((KV_HEADS, 2, rows, HEAD_DIM), BF16),
            pltpu.VMEM((KV_HEADS, 2, rows, HEAD_DIM), BF16),
            pltpu.VMEM((KV_HEADS, 2, rows, HEAD_DIM), BF16),
            pltpu.VMEM((8, HEAD_DIM), F32),
            pltpu.VMEM((rounds, 8, 8, HEAD_DIM), F32),
            dma((2 * KV_HEADS, 2)),
            dma((2, KV_HEADS)),
            dma((KV_HEADS,)),
            dma((2 * KV_HEADS,)),
            dma((2 * KV_HEADS,)),
            dma((2 * KV_HEADS,)),
            dma((2 * KV_HEADS,)),
            dma((KV_HEADS,)),
            dma((KV_HEADS,)),
            dma((KV_HEADS,)),
            dma((KV_HEADS,)),
            dma((KV_HEADS,)),
            dma((KV_HEADS,)),
            dma((rounds, 8)),
            dma((rounds, 8)),
        ],
        compiler_params=pltpu.CompilerParams(
            collective_id=0, has_side_effects=True, vmem_limit_bytes=60 * 1024 * 1024
        ),
        cost_estimate=pl.CostEstimate(
            flops=8 * 2 * HEADS * rows * span * HEAD_DIM,
            bytes_accessed=6 * 1024 * 1024,
            transcendentals=2 * HEADS * rows * span,
        ),
    )(t_query, t_key, t_value, s_query, s_key, s_value, segment_ids.reshape(count, rows))
    return loss.reshape(()), query_grad, key_grad, value_grad


def solution(mesh):
    spread = P("pipe", "ctx", None)
    return jax.shard_map(
        functools.partial(per_device, mesh.shape["ctx"], mesh.shape["pipe"]),
        mesh=mesh,
        in_specs=(spread,) * 6 + (P(),),
        out_specs=(P(), spread, spread, spread),
        check_vma=False,
    )
```

```python
import functools
import math

import jax
import jax.numpy as jnp
from jax import lax
from jax.experimental import pallas as pl
from jax.experimental.pallas import tpu as pltpu
from jax.sharding import PartitionSpec as P

HEADS = 32
KV_HEADS = 4
HEAD_DIM = 128
GROUP = HEADS // KV_HEADS
WIDE = GROUP * HEAD_DIM
PAIR = 2 * HEAD_DIM
PAIRS = GROUP // 2
TEACHER, STUDENT = 0, 1
NEG_FILL = -1e30
PIECES = 8
MESH = pl.DeviceIdType.MESH
F32 = jnp.float32
BF16 = jnp.bfloat16


def dot(a, b):
    return jnp.dot(a, b, preferred_element_type=F32)


def dot_nt(a, b):
    return lax.dot_general(a, b, (((1,), (1,)), ((), ())), preferred_element_type=F32)


def loss_rounds(count):
    bits = count.bit_length() - 1
    return [list(range(low, min(low + 2, bits))) for low in range(0, bits, 2)]


def kernel(
    count, rows, denominator,
    tq, tk, tv, sq, sk, sv, seg,
    loss_out, qg_out, kg_out, vg_out,
    win, qbuf, bias, weights, outs, rinv, dnorm, delta, dscore, ex_tx, ex_rx, qgrad,
    own_grad, far_grad, txx, rxx, tx2, rx2, loss_acc, loss_buf,
    own_sem, q_sem, qg_sem, far_send, far_recv, near_send, near_recv,
    ex_send, ex_recv, gx_send, gx_recv, g2_send, g2_recv, loss_send, loss_recv,
):
    pipe = lax.axis_index("pipe")
    me = lax.axis_index("ctx")
    odd = lax.rem(me, 2)
    partner = me + 1 - 2 * odd
    has_prev = me >= 2
    has_next = me < count - 2
    scale = HEAD_DIM ** (-0.5)
    to_exp2 = scale * math.log2(math.e)
    rounds = loss_rounds(count)

    def xor(value, mask):
        result = value
        for bit in range(count.bit_length() - 1):
            if mask >> bit & 1:
                here = lax.rem(value // (1 << bit), 2)
                result = result + (1 << bit) * (1 - 2 * here)
        return result

    partners = []
    for number, bits in enumerate(rounds):
        masks = [sum(1 << b for k, b in enumerate(bits) if pick >> k & 1) for pick in range(1 << len(bits))]
        flips = (0, 1) if number == 0 else (0,)
        partners.append([(f, m) for f in flips for m in masks if f or m])

    def member(number):
        bits = rounds[number]
        place = lax.rem(me // (1 << bits[0]), 1 << len(bits))
        if number == 0:
            place = place + pipe * (1 << len(bits))
        return place

    def other(flip, mask):
        return (1 - pipe if flip else pipe, xor(me, mask))

    def own_copy(chunk, which):
        g, model = divmod(chunk, 2)
        source = ((tk, tv), (sk, sv))[model][which]
        return pltpu.make_async_copy(
            source.at[0, :, pl.ds(g * HEAD_DIM, HEAD_DIM)],
            win.at[chunk, which, pl.ds(2 * rows, rows), :],
            own_sem.at[chunk, which],
        )

    def q_copy(g, model):
        return pltpu.make_async_copy(
            (tq, sq)[model].at[0, :, pl.ds(g * WIDE, WIDE)], qbuf.at[model, g], q_sem.at[model, g]
        )

    for chunk in range(2 * KV_HEADS):
        for which in range(2):
            own_copy(chunk, which).start()
    for g in range(KV_HEADS):
        for model in (STUDENT, TEACHER):
            q_copy(g, model).start()

    barrier = pltpu.get_barrier_semaphore()
    greeted = 0
    for number in range(len(rounds)):
        for flip, mask in partners[number]:
            pl.semaphore_signal(barrier, inc=1, device_id=other(flip, mask), device_id_type=MESH)
            greeted += 1

    ahead = lax.rem(me // 2, 2)
    remaining = lax.rem(me - 2 + 4 * ahead + count, count)
    pl.semaphore_signal(barrier, inc=1, device_id=(pipe, remaining), device_id_type=MESH)
    greeted += 1

    query_seg = seg[pl.ds(me, 1), :].astype(F32)
    query_pos = lax.broadcasted_iota(jnp.int32, (rows, rows), 1)
    key_pos = lax.broadcasted_iota(jnp.int32, (rows, rows), 0)

    def fill_of(behind):
        source = jnp.maximum(me - behind, 0)
        key_seg = jnp.broadcast_to(seg[pl.ds(source, 1), :].astype(F32), (rows, rows)).T
        fill = jnp.where(key_seg == query_seg, 0.0, NEG_FILL)
        return jnp.where(me >= behind, fill, NEG_FILL)

    bias[pl.ds(0, rows), :] = fill_of(1)
    bias[pl.ds(rows, rows), :] = jnp.where(key_pos <= query_pos, fill_of(0), fill_of(2))

    @pl.when(me < 2)
    def _():
        win[:, :, pl.ds(0, rows), :] = jnp.zeros((2 * KV_HEADS, 2, rows, HEAD_DIM), BF16)

    loss_acc[...] = jnp.zeros_like(loss_acc)
    pl.semaphore_wait(barrier, greeted)

    def far_copy(chunk):
        return pltpu.make_async_remote_copy(
            src_ref=win.at[chunk, :, pl.ds(2 * rows, rows), :],
            dst_ref=win.at[chunk, :, pl.ds(0, rows), :],
            send_sem=far_send.at[chunk],
            recv_sem=far_recv.at[chunk],
            device_id=(pipe, me + 2),
            device_id_type=MESH,
        )

    def near_copy(chunk, slot):
        return pltpu.make_async_remote_copy(
            src_ref=win.at[chunk, :, pl.ds(slot * rows, rows), :],
            dst_ref=win.at[chunk, :, pl.ds(rows, rows), :],
            send_sem=near_send.at[chunk],
            recv_sem=near_recv.at[chunk],
            device_id=(pipe, partner),
            device_id_type=MESH,
        )

    for g in range(KV_HEADS):
        for model in (STUDENT, TEACHER):
            chunk = 2 * g + model
            own_copy(chunk, 0).wait()
            own_copy(chunk, 1).wait()

            @pl.when(has_next)
            def _():
                far_copy(chunk).start()

            @pl.when(odd == 0)
            def _():
                near_copy(chunk, 2).start()

    def ex_copy(g):
        return pltpu.make_async_remote_copy(
            src_ref=ex_tx.at[g], dst_ref=ex_rx.at[g], send_sem=ex_send.at[g], recv_sem=ex_recv.at[g],
            device_id=(1 - pipe, me), device_id_type=MESH,
        )

    def gx_copy(g):
        return pltpu.make_async_remote_copy(
            src_ref=txx.at[g], dst_ref=rxx.at[g], send_sem=gx_send.at[g], recv_sem=gx_recv.at[g],
            device_id=(pipe, partner), device_id_type=MESH,
        )

    def g2_copy(g):
        return pltpu.make_async_remote_copy(
            src_ref=tx2.at[g], dst_ref=rx2.at[g], send_sem=g2_send.at[g], recv_sem=g2_recv.at[g],
            device_id=(pipe, me - 2), device_id_type=MESH,
        )

    def qg_copy(g):
        return pltpu.make_async_copy(
            qgrad.at[g], qg_out.at[0, :, pl.ds(pl.multiple_of(g * WIDE, WIDE), WIDE)], qg_sem.at[g]
        )

    def loss_copy(number, index):
        flip, mask = partners[number][index]
        mine = member(number)
        return pltpu.make_async_remote_copy(
            src_ref=loss_buf.at[number, mine],
            dst_ref=loss_buf.at[number, mine],
            send_sem=loss_send.at[number, index],
            recv_sem=loss_recv.at[number, index],
            device_id=other(flip, mask),
            device_id_type=MESH,
        )

    def loss_start(number, value):
        loss_buf[number, member(number)] = value
        for index in range(len(partners[number])):
            loss_copy(number, index).start()

    def loss_finish(number):
        for index in range(len(partners[number])):
            loss_copy(number, index).wait()
        total = loss_buf[number, 0]
        for place in range(1, len(partners[number]) + 1):
            total = total + loss_buf[number, place]
        return total

    pipe_f = pipe.astype(F32)
    odd_f = odd.astype(F32)

    def query_pair(model, g, hp):
        first = qbuf[model, g, :, pl.ds(hp * PAIR, HEAD_DIM)]
        second = qbuf[model, g, :, pl.ds(hp * PAIR + HEAD_DIM, HEAD_DIM)]
        return jnp.concatenate([first, second], axis=0)

    def wide_iota(axis):
        return lax.broadcasted_iota(jnp.int32, (rows, PAIR), axis)

    def forward(g):
        for model in (STUDENT, TEACHER):
            chunk = 2 * g + model

            @pl.when(has_prev)
            def _():
                far_copy(chunk).wait_recv()

            @pl.when(odd == 1)
            def _():
                near_copy(chunk, 0).start()

        def arrive(model):
            near_copy(2 * g + model, 0).wait_recv()
            pltpu.make_async_copy(
                (tq, sq)[model].at[0, :, pl.ds(0, WIDE)], qbuf.at[model, g], q_sem.at[model, g]
            ).wait()

        arrive(STUDENT)
        slot = lax.rem(g, 2)
        triangle = wide_iota(0) <= lax.rem(wide_iota(1), rows)
        steps = [(model, hp) for model in (STUDENT, TEACHER) for hp in range(PAIRS)]

        def raw_scores(model, hp):
            return dot_nt(win[2 * g + model, 0], query_pair(model, g, hp))

        def finish(model, hp, mixed, inverse):
            cols = pl.ds(hp * PAIR, PAIR)
            mixed = (mixed * inverse).astype(BF16)
            outs[model, g, :, cols] = mixed
            if model == TEACHER:
                student = outs[STUDENT, g, :, cols].astype(F32)
                ex_tx[g, :, cols] = (student - (1.0 + pipe_f) * mixed.astype(F32)).astype(BF16)

        later = raw_scores(*steps[0])
        pending = None
        for index, (model, hp) in enumerate(steps):
            cols = pl.ds(hp * PAIR, PAIR)
            raw = later
            if index + 1 < len(steps):
                if steps[index + 1][0] != model:
                    arrive(steps[index + 1][0])
                later = raw_scores(*steps[index + 1])
            fill = bias[pl.ds(0, rows), :]
            middle = raw[rows : 2 * rows] + jnp.concatenate([fill, fill], axis=1)
            fill = bias[pl.ds(rows, rows), :]
            edge = jnp.where(triangle, raw[2 * rows :], raw[:rows]) + jnp.concatenate([fill, fill], axis=1)
            peak = jnp.max(jnp.maximum(middle, edge), axis=0, keepdims=True)
            middle = jnp.exp2((middle - peak) * to_exp2)
            edge = jnp.exp2((edge - peak) * to_exp2)
            inverse = 1.0 / jnp.sum(middle + edge, axis=0, keepdims=True)
            half = jnp.concatenate(
                [
                    jnp.where(triangle, 0.0, edge).astype(BF16),
                    middle.astype(BF16),
                    jnp.where(triangle, edge, 0.0).astype(BF16),
                ],
                axis=0,
            )
            if model == STUDENT:
                weights[slot, :, cols] = half
                rinv[g, :, cols] = inverse
            if pending is not None:
                finish(*pending)
            if hp == 0:
                values_t = win[2 * g + model, 1].T
            pending = (model, hp, dot(values_t, half), inverse)
        finish(*pending)
        ex_copy(g).start()

    def backward(g):
        slot = lax.rem(g, 2)
        chunk = 2 * g + STUDENT
        ex_copy(g).wait_recv()
        squares = jnp.zeros((8, PAIR), F32)
        for hp in range(PAIRS):
            cols = pl.ds(hp * PAIR, PAIR)
            student = outs[STUDENT, g, :, cols].astype(F32)
            teacher = outs[TEACHER, g, :, cols].astype(F32)
            taken = ex_rx[g, :, cols].astype(F32)
            apart = student - teacher
            first = taken - teacher
            second = taken + apart
            both = first * first + second * second
            squares = squares + jnp.sum(both.reshape(HEAD_DIM // 8, 8, PAIR), axis=0)
            grad = ((2.0 - pipe_f) * apart + taken) * rinv[g, :, cols]
            grad = grad.astype(BF16)
            dnorm[:, cols] = grad
            delta[:, cols] = jnp.sum(grad.astype(F32) * student, axis=0, keepdims=True)
        loss_acc[...] += pipe_f * (squares[:, :HEAD_DIM] + squares[:, HEAD_DIM:])

        @pl.when(g == KV_HEADS - 1)
        def _():
            loss_start(0, loss_acc[...])

        def dprob_of(hp):
            return dot(win[chunk, 1], dnorm[:, pl.ds(hp * PAIR, PAIR)])

        later = dprob_of(0)
        for hp in range(PAIRS):
            cols = pl.ds(hp * PAIR, PAIR)
            dprob = later
            if hp + 1 < PAIRS:
                later = dprob_of(hp + 1)
            else:
                value_win = dot_nt(weights[slot], dnorm[...])
            dscore[:, cols] = (weights[slot, :, cols].astype(F32) * (dprob - delta[:, cols])).astype(BF16)
        queries = jnp.concatenate(
            [qbuf[STUDENT, g, :, pl.ds(h * HEAD_DIM, HEAD_DIM)] for h in range(GROUP)], axis=0
        )
        key_win = dot(dscore[...], queries) * scale
        for which, grads in enumerate((key_win, value_win)):
            far_grad[g, which] = grads[:rows]
            txx[g, which] = grads[rows : 2 * rows].astype(BF16)
            own_grad[g, which] = grads[2 * rows :]
        gx_copy(g).start()
        keys_t = win[chunk, 0].T
        for hp in range(PAIRS):
            query_t = dot(keys_t, dscore[:, pl.ds(hp * PAIR, PAIR)]) * scale
            qgrad[g, :, pl.ds(hp * PAIR, HEAD_DIM)] = query_t[:, :HEAD_DIM].T
            qgrad[g, :, pl.ds(hp * PAIR + HEAD_DIM, HEAD_DIM)] = query_t[:, HEAD_DIM:].T
        qg_copy(g).start()

    def pass_on(g):
        gx_copy(g).wait_recv()
        tx2[g] = (far_grad[g] + odd_f * rxx[g].astype(F32)).astype(BF16)

        @pl.when(has_prev)
        def _():
            g2_copy(g).start()

    def step(g, carry):
        @pl.when(g < KV_HEADS)
        def _():
            forward(g)

        @pl.when(g >= 1)
        def _():
            backward(g - 1)

        @pl.when(g >= 2)
        def _():
            pass_on(g - 2)

        return carry

    lax.fori_loop(0, KV_HEADS + 1, step, 0)
    pass_on(KV_HEADS - 1)

    @pl.when(me >= count - 2)
    def _():
        rx2[...] = jnp.zeros_like(rx2)

    for number in range(1, len(rounds)):
        loss_start(number, loss_finish(number - 1))
    for g in range(KV_HEADS):
        if g == KV_HEADS - 1:
            loss_out[0, 0] = jnp.sum(loss_finish(len(rounds) - 1)) / denominator

        @pl.when(has_next)
        def _():
            g2_copy(g).wait_recv()

        cols = pl.ds(g * HEAD_DIM, HEAD_DIM)
        for which, out in enumerate((kg_out, vg_out)):
            out[0, :, cols] = (
                own_grad[g, which] + rx2[g, which].astype(F32) + (1.0 - odd_f) * rxx[g, which].astype(F32)
            )

    for chunk in range(2 * KV_HEADS):
        near_copy(chunk, 0).wait_send()

        @pl.when(has_next)
        def _():
            far_copy(chunk).wait_send()

    for g in range(KV_HEADS):
        ex_copy(g).wait_send()
        gx_copy(g).wait_send()
        qg_copy(g).wait()

        @pl.when(has_prev)
        def _():
            g2_copy(g).wait_send()


def hand_over(qg_in, kg_in, vg_in, qg_out, kg_out, vg_out, sems):
    part = qg_in.shape[1] // PIECES
    copies = [
        pltpu.make_async_copy(
            qg_in.at[:, pl.ds(k * part, part), :], qg_out.at[:, pl.ds(k * part, part), :], sems.at[k]
        )
        for k in range(PIECES)
    ]
    copies.append(pltpu.make_async_copy(kg_in, kg_out, sems.at[PIECES]))
    copies.append(pltpu.make_async_copy(vg_in, vg_out, sems.at[PIECES + 1]))
    for copy in copies:
        copy.start()
    for copy in copies:
        copy.wait()


def per_device(count, pipes, t_query, t_key, t_value, s_query, s_key, s_value, segment_ids):
    rows = t_query.shape[1]
    span = 3 * rows
    width = KV_HEADS * HEAD_DIM
    denominator = float(pipes * count * rows * HEADS * HEAD_DIM)
    rounds = len(loss_rounds(count))
    dma = pltpu.SemaphoreType.DMA
    anywhere = pl.BlockSpec(memory_space=pltpu.HBM)
    vmem = pl.BlockSpec(memory_space=pltpu.VMEM)
    loss, query_grad, key_grad, value_grad = pl.pallas_call(
        functools.partial(kernel, count, rows, denominator),
        out_shape=(
            jax.ShapeDtypeStruct((1, 1), F32),
            jax.ShapeDtypeStruct((1, rows, HEADS * HEAD_DIM), F32),
            jax.ShapeDtypeStruct((1, rows, width), F32),
            jax.ShapeDtypeStruct((1, rows, width), F32),
        ),
        in_specs=[anywhere] * 6 + [vmem],
        out_specs=(pl.BlockSpec(memory_space=pltpu.SMEM), anywhere, vmem, vmem),
        scratch_shapes=[
            pltpu.VMEM((2 * KV_HEADS, 2, span, HEAD_DIM), BF16),
            pltpu.VMEM((2, KV_HEADS, rows, WIDE), BF16),
            pltpu.VMEM((2 * rows, rows), F32),
            pltpu.VMEM((2, span, WIDE), BF16),
            pltpu.VMEM((2, KV_HEADS, HEAD_DIM, WIDE), BF16),
            pltpu.VMEM((KV_HEADS, 1, WIDE), F32),
            pltpu.VMEM((HEAD_DIM, WIDE), BF16),
            pltpu.VMEM((1, WIDE), F32),
            pltpu.VMEM((span, WIDE), BF16),
            pltpu.VMEM((KV_HEADS, HEAD_DIM, WIDE), BF16),
            pltpu.VMEM((KV_HEADS, HEAD_DIM, WIDE), BF16),
            pltpu.VMEM((KV_HEADS, rows, WIDE), F32),
            pltpu.VMEM((KV_HEADS, 2, rows, HEAD_DIM), F32),
            pltpu.VMEM((KV_HEADS, 2, rows, HEAD_DIM), F32),
            pltpu.VMEM((KV_HEADS, 2, rows, HEAD_DIM), BF16),
            pltpu.VMEM((KV_HEADS, 2, rows, HEAD_DIM), BF16),
            pltpu.VMEM((KV_HEADS, 2, rows, HEAD_DIM), BF16),
            pltpu.VMEM((KV_HEADS, 2, rows, HEAD_DIM), BF16),
            pltpu.VMEM((8, HEAD_DIM), F32),
            pltpu.VMEM((rounds, 8, 8, HEAD_DIM), F32),
            dma((2 * KV_HEADS, 2)),
            dma((2, KV_HEADS)),
            dma((KV_HEADS,)),
            dma((2 * KV_HEADS,)),
            dma((2 * KV_HEADS,)),
            dma((2 * KV_HEADS,)),
            dma((2 * KV_HEADS,)),
            dma((KV_HEADS,)),
            dma((KV_HEADS,)),
            dma((KV_HEADS,)),
            dma((KV_HEADS,)),
            dma((KV_HEADS,)),
            dma((KV_HEADS,)),
            dma((rounds, 8)),
            dma((rounds, 8)),
        ],
        compiler_params=pltpu.CompilerParams(
            collective_id=0, has_side_effects=True, vmem_limit_bytes=60 * 1024 * 1024
        ),
        cost_estimate=pl.CostEstimate(
            flops=8 * 2 * HEADS * rows * span * HEAD_DIM,
            bytes_accessed=6 * 1024 * 1024,
            transcendentals=2 * HEADS * rows * span,
        ),
    )(t_query, t_key, t_value, s_query, s_key, s_value, segment_ids.reshape(count, rows))
    grads = (query_grad, key_grad, value_grad)
    query_grad, key_grad, value_grad = pl.pallas_call(
        hand_over,
        out_shape=tuple(jax.ShapeDtypeStruct(grad.shape, F32) for grad in grads),
        in_specs=[pl.BlockSpec(memory_space=pl.ANY)] * 3,
        out_specs=(anywhere,) * 3,
        scratch_shapes=[dma((PIECES + 2,))],
        compiler_params=pltpu.CompilerParams(vmem_limit_bytes=63 * 1024 * 1024),
    )(*grads)
    return loss.reshape(()), query_grad, key_grad, value_grad


def solution(mesh):
    spread = P("pipe", "ctx", None)
    return jax.shard_map(
        functools.partial(per_device, mesh.shape["ctx"], mesh.shape["pipe"]),
        mesh=mesh,
        in_specs=(spread,) * 6 + (P(),),
        out_specs=(P(), spread, spread, spread),
        check_vma=False,
    )
```

```python
import functools
import math

import jax
import jax.numpy as jnp
from jax import lax
from jax.experimental import pallas as pl
from jax.experimental.pallas import tpu as pltpu
from jax.sharding import PartitionSpec as P

HEADS = 32
KV_HEADS = 4
HEAD_DIM = 128
GROUP = HEADS // KV_HEADS
WIDE = GROUP * HEAD_DIM
PAIR = 2 * HEAD_DIM
PAIRS = GROUP // 2
TEACHER, STUDENT = 0, 1
NEG_FILL = -1e30
PIECES = 8
MESH = pl.DeviceIdType.MESH
F32 = jnp.float32
BF16 = jnp.bfloat16


def dot(a, b):
    return jnp.dot(a, b, preferred_element_type=F32)


def dot_nt(a, b):
    return lax.dot_general(a, b, (((1,), (1,)), ((), ())), preferred_element_type=F32)


def loss_rounds(count):
    bits = count.bit_length() - 1
    return [list(range(low, min(low + 2, bits))) for low in range(0, bits, 2)]


def kernel(
    count, rows, denominator,
    tq, tk, tv, sq, sk, sv, seg,
    loss_out, qg_out, kg_out, vg_out,
    win, qbuf, bias, weights, outs, rinv, dnorm, delta, dscore, ex_tx, ex_rx, qgrad,
    own_grad, far_grad, txx, rxx, tx2, rx2, loss_acc, loss_buf,
    own_sem, q_sem, qg_sem, far_send, far_recv, near_send, near_recv,
    ex_send, ex_recv, gx_send, gx_recv, g2_send, g2_recv, loss_send, loss_recv,
):
    pipe = lax.axis_index("pipe")
    me = lax.axis_index("ctx")
    odd = lax.rem(me, 2)
    partner = me + 1 - 2 * odd
    has_prev = me >= 2
    has_next = me < count - 2
    scale = HEAD_DIM ** (-0.5)
    to_exp2 = scale * math.log2(math.e)
    rounds = loss_rounds(count)

    def xor(value, mask):
        result = value
        for bit in range(count.bit_length() - 1):
            if mask >> bit & 1:
                here = lax.rem(value // (1 << bit), 2)
                result = result + (1 << bit) * (1 - 2 * here)
        return result

    partners = []
    for number, bits in enumerate(rounds):
        masks = [sum(1 << b for k, b in enumerate(bits) if pick >> k & 1) for pick in range(1 << len(bits))]
        flips = (0, 1) if number == 0 else (0,)
        partners.append([(f, m) for f in flips for m in masks if f or m])

    def member(number):
        bits = rounds[number]
        place = lax.rem(me // (1 << bits[0]), 1 << len(bits))
        if number == 0:
            place = place + pipe * (1 << len(bits))
        return place

    def other(flip, mask):
        return (1 - pipe if flip else pipe, xor(me, mask))

    def own_copy(chunk, which):
        g, model = divmod(chunk, 2)
        source = ((tk, tv), (sk, sv))[model][which]
        return pltpu.make_async_copy(
            source.at[0, :, pl.ds(g * HEAD_DIM, HEAD_DIM)],
            win.at[chunk, which, pl.ds(2 * rows, rows), :],
            own_sem.at[chunk, which],
        )

    def q_copy(g, model):
        return pltpu.make_async_copy(
            (tq, sq)[model].at[0, :, pl.ds(g * WIDE, WIDE)], qbuf.at[model, g], q_sem.at[model, g]
        )

    for chunk in range(2 * KV_HEADS):
        for which in range(2):
            own_copy(chunk, which).start()
    for g in range(KV_HEADS):
        for model in (STUDENT, TEACHER):
            q_copy(g, model).start()

    barrier = pltpu.get_barrier_semaphore()
    greeted = 0
    for number in range(len(rounds)):
        for flip, mask in partners[number]:
            pl.semaphore_signal(barrier, inc=1, device_id=other(flip, mask), device_id_type=MESH)
            greeted += 1

    ahead = lax.rem(me // 2, 2)
    remaining = lax.rem(me - 2 + 4 * ahead + count, count)
    pl.semaphore_signal(barrier, inc=1, device_id=(pipe, remaining), device_id_type=MESH)
    greeted += 1

    query_seg = seg[pl.ds(me, 1), :].astype(F32)
    query_pos = lax.broadcasted_iota(jnp.int32, (rows, rows), 1)
    key_pos = lax.broadcasted_iota(jnp.int32, (rows, rows), 0)

    def fill_of(behind):
        source = jnp.maximum(me - behind, 0)
        key_seg = jnp.broadcast_to(seg[pl.ds(source, 1), :].astype(F32), (rows, rows)).T
        fill = jnp.where(key_seg == query_seg, 0.0, NEG_FILL)
        return jnp.where(me >= behind, fill, NEG_FILL)

    bias[pl.ds(0, rows), :] = fill_of(1)
    bias[pl.ds(rows, rows), :] = jnp.where(key_pos <= query_pos, fill_of(0), fill_of(2))

    @pl.when(me < 2)
    def _():
        win[:, :, pl.ds(0, rows), :] = jnp.zeros((2 * KV_HEADS, 2, rows, HEAD_DIM), BF16)

    loss_acc[...] = jnp.zeros_like(loss_acc)
    pl.semaphore_wait(barrier, greeted)

    def far_copy(chunk):
        return pltpu.make_async_remote_copy(
            src_ref=win.at[chunk, :, pl.ds(2 * rows, rows), :],
            dst_ref=win.at[chunk, :, pl.ds(0, rows), :],
            send_sem=far_send.at[chunk],
            recv_sem=far_recv.at[chunk],
            device_id=(pipe, me + 2),
            device_id_type=MESH,
        )

    def near_copy(chunk, slot):
        return pltpu.make_async_remote_copy(
            src_ref=win.at[chunk, :, pl.ds(slot * rows, rows), :],
            dst_ref=win.at[chunk, :, pl.ds(rows, rows), :],
            send_sem=near_send.at[chunk],
            recv_sem=near_recv.at[chunk],
            device_id=(pipe, partner),
            device_id_type=MESH,
        )

    for g in range(KV_HEADS):
        for model in (STUDENT, TEACHER):
            chunk = 2 * g + model
            own_copy(chunk, 0).wait()
            own_copy(chunk, 1).wait()

            @pl.when(has_next)
            def _():
                far_copy(chunk).start()

            @pl.when(odd == 0)
            def _():
                near_copy(chunk, 2).start()

    def ex_copy(g):
        return pltpu.make_async_remote_copy(
            src_ref=ex_tx.at[g], dst_ref=ex_rx.at[g], send_sem=ex_send.at[g], recv_sem=ex_recv.at[g],
            device_id=(1 - pipe, me), device_id_type=MESH,
        )

    def gx_copy(g, which):
        return pltpu.make_async_remote_copy(
            src_ref=txx.at[g, which], dst_ref=rxx.at[g, which],
            send_sem=gx_send.at[g, which], recv_sem=gx_recv.at[g, which],
            device_id=(pipe, partner), device_id_type=MESH,
        )

    def g2_copy(g, which):
        return pltpu.make_async_remote_copy(
            src_ref=tx2.at[g, which], dst_ref=rx2.at[g, which],
            send_sem=g2_send.at[g, which], recv_sem=g2_recv.at[g, which],
            device_id=(pipe, me - 2), device_id_type=MESH,
        )

    def qg_copy(g):
        return pltpu.make_async_copy(
            qgrad.at[g], qg_out.at[0, :, pl.ds(pl.multiple_of(g * WIDE, WIDE), WIDE)], qg_sem.at[g]
        )

    def loss_copy(number, index):
        flip, mask = partners[number][index]
        mine = member(number)
        return pltpu.make_async_remote_copy(
            src_ref=loss_buf.at[number, mine],
            dst_ref=loss_buf.at[number, mine],
            send_sem=loss_send.at[number, index],
            recv_sem=loss_recv.at[number, index],
            device_id=other(flip, mask),
            device_id_type=MESH,
        )

    def loss_start(number, value):
        loss_buf[number, member(number)] = value
        for index in range(len(partners[number])):
            loss_copy(number, index).start()

    def loss_finish(number):
        for index in range(len(partners[number])):
            loss_copy(number, index).wait()
        total = loss_buf[number, 0]
        for place in range(1, len(partners[number]) + 1):
            total = total + loss_buf[number, place]
        return total

    pipe_f = pipe.astype(F32)
    odd_f = odd.astype(F32)

    def query_pair(model, g, hp):
        first = qbuf[model, g, :, pl.ds(hp * PAIR, HEAD_DIM)]
        second = qbuf[model, g, :, pl.ds(hp * PAIR + HEAD_DIM, HEAD_DIM)]
        return jnp.concatenate([first, second], axis=0)

    def wide_iota(axis):
        return lax.broadcasted_iota(jnp.int32, (rows, PAIR), axis)

    def forward(g):
        for model in (STUDENT, TEACHER):
            chunk = 2 * g + model

            @pl.when(has_prev)
            def _():
                far_copy(chunk).wait_recv()

            @pl.when(odd == 1)
            def _():
                near_copy(chunk, 0).start()

        def arrive(model):
            near_copy(2 * g + model, 0).wait_recv()
            pltpu.make_async_copy(
                (tq, sq)[model].at[0, :, pl.ds(0, WIDE)], qbuf.at[model, g], q_sem.at[model, g]
            ).wait()

        arrive(STUDENT)
        slot = lax.rem(g, 2)
        triangle = wide_iota(0) <= lax.rem(wide_iota(1), rows)
        steps = [(model, hp) for model in (STUDENT, TEACHER) for hp in range(PAIRS)]

        def raw_scores(model, hp):
            return dot_nt(win[2 * g + model, 0], query_pair(model, g, hp))

        def finish(model, hp, mixed, inverse):
            cols = pl.ds(hp * PAIR, PAIR)
            mixed = (mixed * inverse).astype(BF16)
            outs[model, g, :, cols] = mixed
            if model == TEACHER:
                student = outs[STUDENT, g, :, cols].astype(F32)
                ex_tx[g, :, cols] = (student - (1.0 + pipe_f) * mixed.astype(F32)).astype(BF16)

        later = raw_scores(*steps[0])
        pending = None
        for index, (model, hp) in enumerate(steps):
            cols = pl.ds(hp * PAIR, PAIR)
            raw = later
            if index + 1 < len(steps):
                if steps[index + 1][0] != model:
                    arrive(steps[index + 1][0])
                later = raw_scores(*steps[index + 1])
            fill = bias[pl.ds(0, rows), :]
            middle = raw[rows : 2 * rows] + jnp.concatenate([fill, fill], axis=1)
            fill = bias[pl.ds(rows, rows), :]
            edge = jnp.where(triangle, raw[2 * rows :], raw[:rows]) + jnp.concatenate([fill, fill], axis=1)
            peak = jnp.max(jnp.maximum(middle, edge), axis=0, keepdims=True)
            middle = jnp.exp2((middle - peak) * to_exp2)
            edge = jnp.exp2((edge - peak) * to_exp2)
            inverse = 1.0 / jnp.sum(middle + edge, axis=0, keepdims=True)
            half = jnp.concatenate(
                [
                    jnp.where(triangle, 0.0, edge).astype(BF16),
                    middle.astype(BF16),
                    jnp.where(triangle, edge, 0.0).astype(BF16),
                ],
                axis=0,
            )
            if model == STUDENT:
                weights[slot, :, cols] = half
                rinv[g, :, cols] = inverse
            if pending is not None:
                finish(*pending)
            if hp == 0:
                values_t = win[2 * g + model, 1].T
            pending = (model, hp, dot(values_t, half), inverse)
        finish(*pending)
        ex_copy(g).start()

    def pass_on(g):
        for which in (1, 0):
            gx_copy(g, which).wait_recv()
            tx2[g, which] = (far_grad[g, which] + odd_f * rxx[g, which].astype(F32)).astype(BF16)

            @pl.when(has_prev)
            def _():
                g2_copy(g, which).start()

    def backward(g):
        slot = lax.rem(g, 2)
        chunk = 2 * g + STUDENT
        ex_copy(g).wait_recv()
        squares = jnp.zeros((8, PAIR), F32)
        for hp in range(PAIRS):
            cols = pl.ds(hp * PAIR, PAIR)
            student = outs[STUDENT, g, :, cols].astype(F32)
            teacher = outs[TEACHER, g, :, cols].astype(F32)
            taken = ex_rx[g, :, cols].astype(F32)
            apart = student - teacher
            first = taken - teacher
            second = taken + apart
            both = first * first + second * second
            squares = squares + jnp.sum(both.reshape(HEAD_DIM // 8, 8, PAIR), axis=0)
            grad = ((2.0 - pipe_f) * apart + taken) * rinv[g, :, cols]
            grad = grad.astype(BF16)
            dnorm[:, cols] = grad
            delta[:, cols] = jnp.sum(grad.astype(F32) * student, axis=0, keepdims=True)
        loss_acc[...] += pipe_f * (squares[:, :HEAD_DIM] + squares[:, HEAD_DIM:])

        @pl.when(g == KV_HEADS - 1)
        def _():
            loss_start(0, loss_acc[...])

        def dprob_of(hp):
            return dot(win[chunk, 1], dnorm[:, pl.ds(hp * PAIR, PAIR)])

        def split(which, grads):
            txx[g, which] = grads[rows : 2 * rows].astype(BF16)
            gx_copy(g, which).start()
            far_grad[g, which] = grads[:rows]
            own_grad[g, which] = grads[2 * rows :]

        later = dprob_of(0)
        split(1, dot_nt(weights[slot], dnorm[...]))

        @pl.when(g >= 1)
        def _():
            pass_on(g - 1)

        for hp in range(PAIRS):
            cols = pl.ds(hp * PAIR, PAIR)
            dprob = later
            if hp + 1 < PAIRS:
                later = dprob_of(hp + 1)
            dscore[:, cols] = (weights[slot, :, cols].astype(F32) * (dprob - delta[:, cols])).astype(BF16)
        queries = jnp.concatenate(
            [qbuf[STUDENT, g, :, pl.ds(h * HEAD_DIM, HEAD_DIM)] for h in range(GROUP)], axis=0
        )
        split(0, dot(dscore[...], queries) * scale)
        keys_t = win[chunk, 0].T
        for hp in range(PAIRS):
            query_t = dot(keys_t, dscore[:, pl.ds(hp * PAIR, PAIR)]) * scale
            qgrad[g, :, pl.ds(hp * PAIR, HEAD_DIM)] = query_t[:, :HEAD_DIM].T
            qgrad[g, :, pl.ds(hp * PAIR + HEAD_DIM, HEAD_DIM)] = query_t[:, HEAD_DIM:].T
        qg_copy(g).start()

    def step(g, carry):
        @pl.when(g < KV_HEADS)
        def _():
            forward(g)

        @pl.when(g >= 1)
        def _():
            backward(g - 1)

        return carry

    lax.fori_loop(0, KV_HEADS + 1, step, 0)
    pass_on(KV_HEADS - 1)

    @pl.when(me >= count - 2)
    def _():
        rx2[...] = jnp.zeros_like(rx2)

    for number in range(1, len(rounds)):
        loss_start(number, loss_finish(number - 1))
    for g in range(KV_HEADS):
        if g == KV_HEADS - 1:
            loss_out[0, 0] = jnp.sum(loss_finish(len(rounds) - 1)) / denominator

        @pl.when(has_next)
        def _():
            g2_copy(g, 0).wait_recv()
            g2_copy(g, 1).wait_recv()

        cols = pl.ds(g * HEAD_DIM, HEAD_DIM)
        for which, out in enumerate((kg_out, vg_out)):
            out[0, :, cols] = (
                own_grad[g, which] + rx2[g, which].astype(F32) + (1.0 - odd_f) * rxx[g, which].astype(F32)
            )

    for chunk in range(2 * KV_HEADS):
        near_copy(chunk, 0).wait_send()

        @pl.when(has_next)
        def _():
            far_copy(chunk).wait_send()

    for g in range(KV_HEADS):
        ex_copy(g).wait_send()
        gx_copy(g, 0).wait_send()
        gx_copy(g, 1).wait_send()
        qg_copy(g).wait()

        @pl.when(has_prev)
        def _():
            g2_copy(g, 0).wait_send()
            g2_copy(g, 1).wait_send()


def hand_over(qg_in, kg_in, vg_in, qg_out, kg_out, vg_out, qg_held, kg_held, vg_held, sems_in, sems_out):
    part = qg_in.shape[1] // PIECES
    rows_of = [pl.ds(k * part, part) for k in range(PIECES)]
    ways = [(qg_in.at[:, r, :], qg_held.at[:, r, :], qg_out.at[:, r, :]) for r in rows_of]
    ways += [(kg_in, kg_held, kg_out), (vg_in, vg_held, vg_out)]
    loads = [pltpu.make_async_copy(src, held, sems_in.at[k]) for k, (src, held, _) in enumerate(ways)]
    stores = [pltpu.make_async_copy(held, dst, sems_out.at[k]) for k, (_, held, dst) in enumerate(ways)]
    for load in loads:
        load.start()
    for load, store in zip(loads, stores):
        load.wait()
        store.start()
    for store in stores:
        store.wait()


def per_device(count, pipes, t_query, t_key, t_value, s_query, s_key, s_value, segment_ids):
    rows = t_query.shape[1]
    span = 3 * rows
    width = KV_HEADS * HEAD_DIM
    denominator = float(pipes * count * rows * HEADS * HEAD_DIM)
    rounds = len(loss_rounds(count))
    dma = pltpu.SemaphoreType.DMA
    anywhere = pl.BlockSpec(memory_space=pltpu.HBM)
    vmem = pl.BlockSpec(memory_space=pltpu.VMEM)
    loss, query_grad, key_grad, value_grad = pl.pallas_call(
        functools.partial(kernel, count, rows, denominator),
        out_shape=(
            jax.ShapeDtypeStruct((1, 1), F32),
            jax.ShapeDtypeStruct((1, rows, HEADS * HEAD_DIM), F32),
            jax.ShapeDtypeStruct((1, rows, width), F32),
            jax.ShapeDtypeStruct((1, rows, width), F32),
        ),
        in_specs=[anywhere] * 6 + [vmem],
        out_specs=(pl.BlockSpec(memory_space=pltpu.SMEM), anywhere, vmem, vmem),
        scratch_shapes=[
            pltpu.VMEM((2 * KV_HEADS, 2, span, HEAD_DIM), BF16),
            pltpu.VMEM((2, KV_HEADS, rows, WIDE), BF16),
            pltpu.VMEM((2 * rows, rows), F32),
            pltpu.VMEM((2, span, WIDE), BF16),
            pltpu.VMEM((2, KV_HEADS, HEAD_DIM, WIDE), BF16),
            pltpu.VMEM((KV_HEADS, 1, WIDE), F32),
            pltpu.VMEM((HEAD_DIM, WIDE), BF16),
            pltpu.VMEM((1, WIDE), F32),
            pltpu.VMEM((span, WIDE), BF16),
            pltpu.VMEM((KV_HEADS, HEAD_DIM, WIDE), BF16),
            pltpu.VMEM((KV_HEADS, HEAD_DIM, WIDE), BF16),
            pltpu.VMEM((KV_HEADS, rows, WIDE), F32),
            pltpu.VMEM((KV_HEADS, 2, rows, HEAD_DIM), F32),
            pltpu.VMEM((KV_HEADS, 2, rows, HEAD_DIM), F32),
            pltpu.VMEM((KV_HEADS, 2, rows, HEAD_DIM), BF16),
            pltpu.VMEM((KV_HEADS, 2, rows, HEAD_DIM), BF16),
            pltpu.VMEM((KV_HEADS, 2, rows, HEAD_DIM), BF16),
            pltpu.VMEM((KV_HEADS, 2, rows, HEAD_DIM), BF16),
            pltpu.VMEM((8, HEAD_DIM), F32),
            pltpu.VMEM((rounds, 8, 8, HEAD_DIM), F32),
            dma((2 * KV_HEADS, 2)),
            dma((2, KV_HEADS)),
            dma((KV_HEADS,)),
            dma((2 * KV_HEADS,)),
            dma((2 * KV_HEADS,)),
            dma((2 * KV_HEADS,)),
            dma((2 * KV_HEADS,)),
            dma((KV_HEADS,)),
            dma((KV_HEADS,)),
            dma((KV_HEADS, 2)),
            dma((KV_HEADS, 2)),
            dma((KV_HEADS, 2)),
            dma((KV_HEADS, 2)),
            dma((rounds, 8)),
            dma((rounds, 8)),
        ],
        compiler_params=pltpu.CompilerParams(
            collective_id=0, has_side_effects=True, vmem_limit_bytes=60 * 1024 * 1024
        ),
        cost_estimate=pl.CostEstimate(
            flops=8 * 2 * HEADS * rows * span * HEAD_DIM,
            bytes_accessed=6 * 1024 * 1024,
            transcendentals=2 * HEADS * rows * span,
        ),
    )(t_query, t_key, t_value, s_query, s_key, s_value, segment_ids.reshape(count, rows))
    grads = (query_grad, key_grad, value_grad)
    query_grad, key_grad, value_grad = pl.pallas_call(
        hand_over,
        out_shape=tuple(jax.ShapeDtypeStruct(grad.shape, F32) for grad in grads),
        in_specs=[pl.BlockSpec(memory_space=pl.ANY)] * 3,
        out_specs=(anywhere,) * 3,
        scratch_shapes=[pltpu.VMEM(grad.shape, F32) for grad in grads] + [dma((PIECES + 2,))] * 2,
        compiler_params=pltpu.CompilerParams(vmem_limit_bytes=63 * 1024 * 1024),
    )(*grads)
    return loss.reshape(()), query_grad, key_grad, value_grad


def solution(mesh):
    spread = P("pipe", "ctx", None)
    return jax.shard_map(
        functools.partial(per_device, mesh.shape["ctx"], mesh.shape["pipe"]),
        mesh=mesh,
        in_specs=(spread,) * 6 + (P(),),
        out_specs=(P(), spread, spread, spread),
        check_vma=False,
    )
```

```python
import functools
import math

import jax
import jax.numpy as jnp
from jax import lax
from jax.experimental import pallas as pl
from jax.experimental.pallas import tpu as pltpu
from jax.sharding import PartitionSpec as P

HEADS = 32
KV_HEADS = 4
HEAD_DIM = 128
GROUP = HEADS // KV_HEADS
WIDE = GROUP * HEAD_DIM
PAIR = 2 * HEAD_DIM
PAIRS = GROUP // 2
TEACHER, STUDENT = 0, 1
NEG_FILL = -1e30
PIECES = 8
MESH = pl.DeviceIdType.MESH
F32 = jnp.float32
BF16 = jnp.bfloat16


def dot(a, b):
    return jnp.dot(a, b, preferred_element_type=F32)


def dot_nt(a, b):
    return lax.dot_general(a, b, (((1,), (1,)), ((), ())), preferred_element_type=F32)


def loss_rounds(count):
    bits = count.bit_length() - 1
    return [list(range(low, min(low + 2, bits))) for low in range(0, bits, 2)]


def kernel(
    count, rows, denominator,
    tq, tk, tv, sq, sk, sv, seg,
    loss_out, qg_out, kg_out, vg_out,
    win, qbuf, bias, weights, outs, rinv, dnorm, delta, dscore, ex_tx, ex_rx, qgrad,
    own_grad, far_grad, txx, rxx, tx2, rx2, loss_acc, loss_buf,
    own_sem, q_sem, qg_sem, far_send, far_recv, near_send, near_recv,
    ex_send, ex_recv, gx_send, gx_recv, g2_send, g2_recv, loss_send, loss_recv,
):
    pipe = lax.axis_index("pipe")
    me = lax.axis_index("ctx")
    odd = lax.rem(me, 2)
    partner = me + 1 - 2 * odd
    has_prev = me >= 2
    has_next = me < count - 2
    scale = HEAD_DIM ** (-0.5)
    to_exp2 = scale * math.log2(math.e)
    rounds = loss_rounds(count)

    def xor(value, mask):
        result = value
        for bit in range(count.bit_length() - 1):
            if mask >> bit & 1:
                here = lax.rem(value // (1 << bit), 2)
                result = result + (1 << bit) * (1 - 2 * here)
        return result

    partners = []
    for number, bits in enumerate(rounds):
        masks = [sum(1 << b for k, b in enumerate(bits) if pick >> k & 1) for pick in range(1 << len(bits))]
        flips = (0, 1) if number == 0 else (0,)
        partners.append([(f, m) for f in flips for m in masks if f or m])

    def member(number):
        bits = rounds[number]
        place = lax.rem(me // (1 << bits[0]), 1 << len(bits))
        if number == 0:
            place = place + pipe * (1 << len(bits))
        return place

    def other(flip, mask):
        return (1 - pipe if flip else pipe, xor(me, mask))

    def own_copy(chunk, which):
        g, model = divmod(chunk, 2)
        source = ((tk, tv), (sk, sv))[model][which]
        return pltpu.make_async_copy(
            source.at[0, :, pl.ds(g * HEAD_DIM, HEAD_DIM)],
            win.at[chunk, which, pl.ds(2 * rows, rows), :],
            own_sem.at[chunk, which],
        )

    def q_copy(g, model):
        return pltpu.make_async_copy(
            (tq, sq)[model].at[0, :, pl.ds(g * WIDE, WIDE)], qbuf.at[model, g], q_sem.at[model, g]
        )

    for chunk in range(2 * KV_HEADS):
        for which in range(2):
            own_copy(chunk, which).start()
    for g in range(KV_HEADS):
        for model in (STUDENT, TEACHER):
            q_copy(g, model).start()

    barrier = pltpu.get_barrier_semaphore()
    greeted = 0
    for number in range(len(rounds)):
        for flip, mask in partners[number]:
            pl.semaphore_signal(barrier, inc=1, device_id=other(flip, mask), device_id_type=MESH)
            greeted += 1

    ahead = lax.rem(me // 2, 2)
    remaining = lax.rem(me - 2 + 4 * ahead + count, count)
    pl.semaphore_signal(barrier, inc=1, device_id=(pipe, remaining), device_id_type=MESH)
    greeted += 1

    query_seg = seg[pl.ds(me, 1), :].astype(F32)
    query_pos = lax.broadcasted_iota(jnp.int32, (rows, rows), 1)
    key_pos = lax.broadcasted_iota(jnp.int32, (rows, rows), 0)

    def fill_of(behind):
        source = jnp.maximum(me - behind, 0)
        key_seg = jnp.broadcast_to(seg[pl.ds(source, 1), :].astype(F32), (rows, rows)).T
        fill = jnp.where(key_seg == query_seg, 0.0, NEG_FILL)
        return jnp.where(me >= behind, fill, NEG_FILL)

    bias[pl.ds(0, rows), :] = fill_of(1)
    bias[pl.ds(rows, rows), :] = jnp.where(key_pos <= query_pos, fill_of(0), fill_of(2))

    @pl.when(me < 2)
    def _():
        win[:, :, pl.ds(0, rows), :] = jnp.zeros((2 * KV_HEADS, 2, rows, HEAD_DIM), BF16)

    loss_acc[...] = jnp.zeros_like(loss_acc)
    pl.semaphore_wait(barrier, greeted)

    def far_copy(chunk):
        return pltpu.make_async_remote_copy(
            src_ref=win.at[chunk, :, pl.ds(2 * rows, rows), :],
            dst_ref=win.at[chunk, :, pl.ds(0, rows), :],
            send_sem=far_send.at[chunk],
            recv_sem=far_recv.at[chunk],
            device_id=(pipe, me + 2),
            device_id_type=MESH,
        )

    def near_copy(chunk, slot):
        return pltpu.make_async_remote_copy(
            src_ref=win.at[chunk, :, pl.ds(slot * rows, rows), :],
            dst_ref=win.at[chunk, :, pl.ds(rows, rows), :],
            send_sem=near_send.at[chunk],
            recv_sem=near_recv.at[chunk],
            device_id=(pipe, partner),
            device_id_type=MESH,
        )

    for g in range(KV_HEADS):
        for model in (STUDENT, TEACHER):
            chunk = 2 * g + model
            own_copy(chunk, 0).wait()
            own_copy(chunk, 1).wait()

            @pl.when(has_next)
            def _():
                far_copy(chunk).start()

            @pl.when(odd == 0)
            def _():
                near_copy(chunk, 2).start()

    def ex_copy(g):
        return pltpu.make_async_remote_copy(
            src_ref=ex_tx.at[g], dst_ref=ex_rx.at[g], send_sem=ex_send.at[g], recv_sem=ex_recv.at[g],
            device_id=(1 - pipe, me), device_id_type=MESH,
        )

    def gx_copy(g):
        return pltpu.make_async_remote_copy(
            src_ref=txx.at[g], dst_ref=rxx.at[g], send_sem=gx_send.at[g], recv_sem=gx_recv.at[g],
            device_id=(pipe, partner), device_id_type=MESH,
        )

    def g2_copy(g):
        return pltpu.make_async_remote_copy(
            src_ref=tx2.at[g], dst_ref=rx2.at[g], send_sem=g2_send.at[g], recv_sem=g2_recv.at[g],
            device_id=(pipe, me - 2), device_id_type=MESH,
        )

    def qg_copy(g):
        return pltpu.make_async_copy(
            qgrad.at[g], qg_out.at[0, :, pl.ds(pl.multiple_of(g * WIDE, WIDE), WIDE)], qg_sem.at[g]
        )

    def loss_copy(number, index):
        flip, mask = partners[number][index]
        mine = member(number)
        return pltpu.make_async_remote_copy(
            src_ref=loss_buf.at[number, mine],
            dst_ref=loss_buf.at[number, mine],
            send_sem=loss_send.at[number, index],
            recv_sem=loss_recv.at[number, index],
            device_id=other(flip, mask),
            device_id_type=MESH,
        )

    def loss_start(number, value):
        loss_buf[number, member(number)] = value
        for index in range(len(partners[number])):
            loss_copy(number, index).start()

    def loss_finish(number):
        for index in range(len(partners[number])):
            loss_copy(number, index).wait()
        total = loss_buf[number, 0]
        for place in range(1, len(partners[number]) + 1):
            total = total + loss_buf[number, place]
        return total

    pipe_f = pipe.astype(F32)
    odd_f = odd.astype(F32)

    def query_pair(model, g, hp):
        first = qbuf[model, g, :, pl.ds(hp * PAIR, HEAD_DIM)]
        second = qbuf[model, g, :, pl.ds(hp * PAIR + HEAD_DIM, HEAD_DIM)]
        return jnp.concatenate([first, second], axis=0)

    def wide_iota(axis):
        return lax.broadcasted_iota(jnp.int32, (rows, PAIR), axis)

    def forward(g):
        for model in (STUDENT, TEACHER):
            chunk = 2 * g + model

            @pl.when(has_prev)
            def _():
                far_copy(chunk).wait_recv()

            @pl.when(odd == 1)
            def _():
                near_copy(chunk, 0).start()

        def arrive(model):
            near_copy(2 * g + model, 0).wait_recv()
            pltpu.make_async_copy(
                (tq, sq)[model].at[0, :, pl.ds(0, WIDE)], qbuf.at[model, g], q_sem.at[model, g]
            ).wait()

        arrive(STUDENT)
        slot = lax.rem(g, 2)
        triangle = wide_iota(0) <= lax.rem(wide_iota(1), rows)
        steps = [(model, hp) for model in (STUDENT, TEACHER) for hp in range(PAIRS)]

        def raw_scores(model, hp):
            return dot_nt(win[2 * g + model, 0], query_pair(model, g, hp))

        def finish(model, hp, mixed, inverse):
            cols = pl.ds(hp * PAIR, PAIR)
            mixed = (mixed * inverse).astype(BF16)
            outs[model, g, :, cols] = mixed
            if model == TEACHER:
                student = outs[STUDENT, g, :, cols].astype(F32)
                ex_tx[g, :, cols] = (student - (1.0 + pipe_f) * mixed.astype(F32)).astype(BF16)

        later = raw_scores(*steps[0])
        pending = None
        for index, (model, hp) in enumerate(steps):
            cols = pl.ds(hp * PAIR, PAIR)
            raw = later
            if index + 1 < len(steps):
                if steps[index + 1][0] != model:
                    arrive(steps[index + 1][0])
                later = raw_scores(*steps[index + 1])
            fill = bias[pl.ds(0, rows), :]
            middle = raw[rows : 2 * rows] + jnp.concatenate([fill, fill], axis=1)
            fill = bias[pl.ds(rows, rows), :]
            edge = jnp.where(triangle, raw[2 * rows :], raw[:rows]) + jnp.concatenate([fill, fill], axis=1)
            peak = jnp.max(jnp.maximum(middle, edge), axis=0, keepdims=True)
            middle = jnp.exp2((middle - peak) * to_exp2)
            edge = jnp.exp2((edge - peak) * to_exp2)
            inverse = 1.0 / jnp.sum(middle + edge, axis=0, keepdims=True)
            half = jnp.concatenate(
                [
                    jnp.where(triangle, 0.0, edge).astype(BF16),
                    middle.astype(BF16),
                    jnp.where(triangle, edge, 0.0).astype(BF16),
                ],
                axis=0,
            )
            if model == STUDENT:
                weights[slot, :, cols] = half
                rinv[g, :, cols] = inverse
            if pending is not None:
                finish(*pending)
            if hp == 0:
                values_t = win[2 * g + model, 1].T
            pending = (model, hp, dot(values_t, half), inverse)
        finish(*pending)
        ex_copy(g).start()

    def backward(g):
        slot = lax.rem(g, 2)
        chunk = 2 * g + STUDENT
        ex_copy(g).wait_recv()
        squares = jnp.zeros((8, PAIR), F32)
        for hp in range(PAIRS):
            cols = pl.ds(hp * PAIR, PAIR)
            student = outs[STUDENT, g, :, cols].astype(F32)
            teacher = outs[TEACHER, g, :, cols].astype(F32)
            taken = ex_rx[g, :, cols].astype(F32)
            apart = student - teacher
            first = taken - teacher
            second = taken + apart
            both = first * first + second * second
            squares = squares + jnp.sum(both.reshape(HEAD_DIM // 8, 8, PAIR), axis=0)
            grad = ((2.0 - pipe_f) * apart + taken) * rinv[g, :, cols]
            grad = grad.astype(BF16)
            dnorm[:, cols] = grad
            delta[:, cols] = jnp.sum(grad.astype(F32) * student, axis=0, keepdims=True)
        loss_acc[...] += pipe_f * (squares[:, :HEAD_DIM] + squares[:, HEAD_DIM:])

        @pl.when(g == KV_HEADS - 1)
        def _():
            loss_start(0, loss_acc[...])

        def dprob_of(hp):
            return dot(win[chunk, 1], dnorm[:, pl.ds(hp * PAIR, PAIR)])

        later = dprob_of(0)
        for hp in range(PAIRS):
            cols = pl.ds(hp * PAIR, PAIR)
            dprob = later
            if hp + 1 < PAIRS:
                later = dprob_of(hp + 1)
            else:
                value_win = dot_nt(weights[slot], dnorm[...])
            dscore[:, cols] = (weights[slot, :, cols].astype(F32) * (dprob - delta[:, cols])).astype(BF16)
        queries = jnp.concatenate(
            [qbuf[STUDENT, g, :, pl.ds(h * HEAD_DIM, HEAD_DIM)] for h in range(GROUP)], axis=0
        )
        key_win = dot(dscore[...], queries) * scale
        for which, grads in enumerate((key_win, value_win)):
            far_grad[g, which] = grads[:rows]
            txx[g, which] = grads[rows : 2 * rows].astype(BF16)
            own_grad[g, which] = grads[2 * rows :]
        gx_copy(g).start()
        keys_t = win[chunk, 0].T
        for hp in range(PAIRS):
            query_t = dot(keys_t, dscore[:, pl.ds(hp * PAIR, PAIR)]) * scale
            qgrad[g, :, pl.ds(hp * PAIR, HEAD_DIM)] = query_t[:, :HEAD_DIM].T
            qgrad[g, :, pl.ds(hp * PAIR + HEAD_DIM, HEAD_DIM)] = query_t[:, HEAD_DIM:].T
        qg_copy(g).start()

    def pass_on(g):
        gx_copy(g).wait_recv()
        tx2[g] = (far_grad[g] + odd_f * rxx[g].astype(F32)).astype(BF16)

        @pl.when(has_prev)
        def _():
            g2_copy(g).start()

    def step(g, carry):
        @pl.when(g < KV_HEADS)
        def _():
            forward(g)

        @pl.when(g >= 1)
        def _():
            backward(g - 1)

        @pl.when(g >= 2)
        def _():
            pass_on(g - 2)

        return carry

    lax.fori_loop(0, KV_HEADS + 1, step, 0)
    pass_on(KV_HEADS - 1)

    @pl.when(me >= count - 2)
    def _():
        rx2[...] = jnp.zeros_like(rx2)

    for number in range(1, len(rounds)):
        loss_start(number, loss_finish(number - 1))
    for g in range(KV_HEADS):
        if g == KV_HEADS - 1:
            loss_out[0, 0] = jnp.sum(loss_finish(len(rounds) - 1)) / denominator

        @pl.when(has_next)
        def _():
            g2_copy(g).wait_recv()

        cols = pl.ds(g * HEAD_DIM, HEAD_DIM)
        for which, out in enumerate((kg_out, vg_out)):
            out[0, :, cols] = (
                own_grad[g, which] + rx2[g, which].astype(F32) + (1.0 - odd_f) * rxx[g, which].astype(F32)
            )

    for chunk in range(2 * KV_HEADS):
        near_copy(chunk, 0).wait_send()

        @pl.when(has_next)
        def _():
            far_copy(chunk).wait_send()

    for g in range(KV_HEADS):
        ex_copy(g).wait_send()
        gx_copy(g).wait_send()
        qg_copy(g).wait()

        @pl.when(has_prev)
        def _():
            g2_copy(g).wait_send()


def hand_over(qg_in, kg_in, vg_in, qg_out, kg_out, vg_out, qg_held, kg_held, vg_held, sems_in, sems_out):
    part = qg_in.shape[1] // PIECES
    rows_of = [pl.ds(k * part, part) for k in range(PIECES)]
    ways = [(qg_in.at[:, r, :], qg_held.at[:, r, :], qg_out.at[:, r, :]) for r in rows_of]
    ways += [(kg_in, kg_held, kg_out), (vg_in, vg_held, vg_out)]
    loads = [pltpu.make_async_copy(src, held, sems_in.at[k]) for k, (src, held, _) in enumerate(ways)]
    stores = [pltpu.make_async_copy(held, dst, sems_out.at[k]) for k, (_, held, dst) in enumerate(ways)]
    for load in loads:
        load.start()
    for load, store in zip(loads, stores):
        load.wait()
        store.start()
    for store in stores:
        store.wait()


def per_device(count, pipes, t_query, t_key, t_value, s_query, s_key, s_value, segment_ids):
    rows = t_query.shape[1]
    span = 3 * rows
    width = KV_HEADS * HEAD_DIM
    denominator = float(pipes * count * rows * HEADS * HEAD_DIM)
    rounds = len(loss_rounds(count))
    dma = pltpu.SemaphoreType.DMA
    anywhere = pl.BlockSpec(memory_space=pltpu.HBM)
    vmem = pl.BlockSpec(memory_space=pltpu.VMEM)
    loss, query_grad, key_grad, value_grad = pl.pallas_call(
        functools.partial(kernel, count, rows, denominator),
        out_shape=(
            jax.ShapeDtypeStruct((1, 1), F32),
            jax.ShapeDtypeStruct((1, rows, HEADS * HEAD_DIM), F32),
            jax.ShapeDtypeStruct((1, rows, width), F32),
            jax.ShapeDtypeStruct((1, rows, width), F32),
        ),
        in_specs=[anywhere] * 6 + [vmem],
        out_specs=(pl.BlockSpec(memory_space=pltpu.SMEM), anywhere, vmem, vmem),
        scratch_shapes=[
            pltpu.VMEM((2 * KV_HEADS, 2, span, HEAD_DIM), BF16),
            pltpu.VMEM((2, KV_HEADS, rows, WIDE), BF16),
            pltpu.VMEM((2 * rows, rows), F32),
            pltpu.VMEM((2, span, WIDE), BF16),
            pltpu.VMEM((2, KV_HEADS, HEAD_DIM, WIDE), BF16),
            pltpu.VMEM((KV_HEADS, 1, WIDE), F32),
            pltpu.VMEM((HEAD_DIM, WIDE), BF16),
            pltpu.VMEM((1, WIDE), F32),
            pltpu.VMEM((span, WIDE), BF16),
            pltpu.VMEM((KV_HEADS, HEAD_DIM, WIDE), BF16),
            pltpu.VMEM((KV_HEADS, HEAD_DIM, WIDE), BF16),
            pltpu.VMEM((KV_HEADS, rows, WIDE), F32),
            pltpu.VMEM((KV_HEADS, 2, rows, HEAD_DIM), F32),
            pltpu.VMEM((KV_HEADS, 2, rows, HEAD_DIM), F32),
            pltpu.VMEM((KV_HEADS, 2, rows, HEAD_DIM), BF16),
            pltpu.VMEM((KV_HEADS, 2, rows, HEAD_DIM), BF16),
            pltpu.VMEM((KV_HEADS, 2, rows, HEAD_DIM), BF16),
            pltpu.VMEM((KV_HEADS, 2, rows, HEAD_DIM), BF16),
            pltpu.VMEM((8, HEAD_DIM), F32),
            pltpu.VMEM((rounds, 8, 8, HEAD_DIM), F32),
            dma((2 * KV_HEADS, 2)),
            dma((2, KV_HEADS)),
            dma((KV_HEADS,)),
            dma((2 * KV_HEADS,)),
            dma((2 * KV_HEADS,)),
            dma((2 * KV_HEADS,)),
            dma((2 * KV_HEADS,)),
            dma((KV_HEADS,)),
            dma((KV_HEADS,)),
            dma((KV_HEADS,)),
            dma((KV_HEADS,)),
            dma((KV_HEADS,)),
            dma((KV_HEADS,)),
            dma((rounds, 8)),
            dma((rounds, 8)),
        ],
        compiler_params=pltpu.CompilerParams(
            collective_id=0, has_side_effects=True, vmem_limit_bytes=60 * 1024 * 1024
        ),
        cost_estimate=pl.CostEstimate(
            flops=8 * 2 * HEADS * rows * span * HEAD_DIM,
            bytes_accessed=6 * 1024 * 1024,
            transcendentals=2 * HEADS * rows * span,
        ),
    )(t_query, t_key, t_value, s_query, s_key, s_value, segment_ids.reshape(count, rows))
    grads = (query_grad, key_grad, value_grad)
    query_grad, key_grad, value_grad = pl.pallas_call(
        hand_over,
        out_shape=tuple(jax.ShapeDtypeStruct(grad.shape, F32) for grad in grads),
        in_specs=[pl.BlockSpec(memory_space=pl.ANY)] * 3,
        out_specs=(anywhere,) * 3,
        scratch_shapes=[pltpu.VMEM(grad.shape, F32) for grad in grads] + [dma((PIECES + 2,))] * 2,
        compiler_params=pltpu.CompilerParams(vmem_limit_bytes=63 * 1024 * 1024),
    )(*grads)
    return loss.reshape(()), query_grad, key_grad, value_grad


def solution(mesh):
    spread = P("pipe", "ctx", None)
    return jax.shard_map(
        functools.partial(per_device, mesh.shape["ctx"], mesh.shape["pipe"]),
        mesh=mesh,
        in_specs=(spread,) * 6 + (P(),),
        out_specs=(P(), spread, spread, spread),
        check_vma=False,
    )
```

```python
import functools
import math

import jax
import jax.numpy as jnp
from jax import lax
from jax.experimental import pallas as pl
from jax.experimental.pallas import tpu as pltpu
from jax.sharding import PartitionSpec as P

HEADS = 32
KV_HEADS = 4
HEAD_DIM = 128
GROUP = HEADS // KV_HEADS
WIDE = GROUP * HEAD_DIM
PAIR = 2 * HEAD_DIM
PAIRS = GROUP // 2
TEACHER, STUDENT = 0, 1
NEG_FILL = -1e30
PIECES = 8
MESH = pl.DeviceIdType.MESH
F32 = jnp.float32
BF16 = jnp.bfloat16


def dot(a, b):
    return jnp.dot(a, b, preferred_element_type=F32)


def dot_nt(a, b):
    return lax.dot_general(a, b, (((1,), (1,)), ((), ())), preferred_element_type=F32)


def loss_rounds(count):
    bits = count.bit_length() - 1
    return [list(range(low, min(low + 2, bits))) for low in range(0, bits, 2)]


def kernel(
    count, rows, denominator,
    tq, tk, tv, sq, sk, sv, seg,
    loss_out, qg_out, kg_out, vg_out,
    win, qbuf, bias, weights, outs, rinv, dnorm, delta, dscore, ex_tx, ex_rx, qgrad,
    own_grad, far_grad, txx, rxx, tx2, rx2, loss_acc, loss_buf,
    own_sem, q_sem, qg_sem, far_send, far_recv, near_send, near_recv,
    ex_send, ex_recv, gx_send, gx_recv, g2_send, g2_recv, loss_send, loss_recv,
):
    pipe = lax.axis_index("pipe")
    me = lax.axis_index("ctx")
    odd = lax.rem(me, 2)
    partner = me + 1 - 2 * odd
    has_prev = me >= 2
    has_next = me < count - 2
    scale = HEAD_DIM ** (-0.5)
    to_exp2 = scale * math.log2(math.e)
    rounds = loss_rounds(count)

    def xor(value, mask):
        result = value
        for bit in range(count.bit_length() - 1):
            if mask >> bit & 1:
                here = lax.rem(value // (1 << bit), 2)
                result = result + (1 << bit) * (1 - 2 * here)
        return result

    partners = []
    for number, bits in enumerate(rounds):
        masks = [sum(1 << b for k, b in enumerate(bits) if pick >> k & 1) for pick in range(1 << len(bits))]
        flips = (0, 1) if number == 0 else (0,)
        partners.append([(f, m) for f in flips for m in masks if f or m])

    def member(number):
        bits = rounds[number]
        place = lax.rem(me // (1 << bits[0]), 1 << len(bits))
        if number == 0:
            place = place + pipe * (1 << len(bits))
        return place

    def other(flip, mask):
        return (1 - pipe if flip else pipe, xor(me, mask))

    def own_copy(chunk, which):
        g, model = divmod(chunk, 2)
        source = ((tk, tv), (sk, sv))[model][which]
        return pltpu.make_async_copy(
            source.at[0, :, pl.ds(g * HEAD_DIM, HEAD_DIM)],
            win.at[chunk, which, pl.ds(2 * rows, rows), :],
            own_sem.at[chunk, which],
        )

    def q_copy(g, model):
        return pltpu.make_async_copy(
            (tq, sq)[model].at[0, :, pl.ds(g * WIDE, WIDE)], qbuf.at[model, g], q_sem.at[model, g]
        )

    for chunk in range(2 * KV_HEADS):
        for which in range(2):
            own_copy(chunk, which).start()
    for g in range(KV_HEADS):
        for model in (STUDENT, TEACHER):
            q_copy(g, model).start()

    barrier = pltpu.get_barrier_semaphore()
    greeted = 0
    for number in range(len(rounds)):
        for flip, mask in partners[number]:
            pl.semaphore_signal(barrier, inc=1, device_id=other(flip, mask), device_id_type=MESH)
            greeted += 1

    ahead = lax.rem(me // 2, 2)
    remaining = lax.rem(me - 2 + 4 * ahead + count, count)
    pl.semaphore_signal(barrier, inc=1, device_id=(pipe, remaining), device_id_type=MESH)
    greeted += 1

    query_seg = seg[pl.ds(me, 1), :].astype(F32)
    query_pos = lax.broadcasted_iota(jnp.int32, (rows, rows), 1)
    key_pos = lax.broadcasted_iota(jnp.int32, (rows, rows), 0)

    def fill_of(behind):
        source = jnp.maximum(me - behind, 0)
        key_seg = jnp.broadcast_to(seg[pl.ds(source, 1), :].astype(F32), (rows, rows)).T
        fill = jnp.where(key_seg == query_seg, 0.0, NEG_FILL)
        return jnp.where(me >= behind, fill, NEG_FILL)

    bias[pl.ds(0, rows), :] = fill_of(1)
    bias[pl.ds(rows, rows), :] = jnp.where(key_pos <= query_pos, fill_of(0), fill_of(2))

    @pl.when(me < 2)
    def _():
        win[:, :, pl.ds(0, rows), :] = jnp.zeros((2 * KV_HEADS, 2, rows, HEAD_DIM), BF16)

    loss_acc[...] = jnp.zeros_like(loss_acc)
    pl.semaphore_wait(barrier, greeted)

    def far_copy(chunk):
        return pltpu.make_async_remote_copy(
            src_ref=win.at[chunk, :, pl.ds(2 * rows, rows), :],
            dst_ref=win.at[chunk, :, pl.ds(0, rows), :],
            send_sem=far_send.at[chunk],
            recv_sem=far_recv.at[chunk],
            device_id=(pipe, me + 2),
            device_id_type=MESH,
        )

    def near_copy(chunk, slot):
        return pltpu.make_async_remote_copy(
            src_ref=win.at[chunk, :, pl.ds(slot * rows, rows), :],
            dst_ref=win.at[chunk, :, pl.ds(rows, rows), :],
            send_sem=near_send.at[chunk],
            recv_sem=near_recv.at[chunk],
            device_id=(pipe, partner),
            device_id_type=MESH,
        )

    for g in range(KV_HEADS):
        for model in (STUDENT, TEACHER):
            chunk = 2 * g + model
            own_copy(chunk, 0).wait()
            own_copy(chunk, 1).wait()

            @pl.when(has_next)
            def _():
                far_copy(chunk).start()

            @pl.when(odd == 0)
            def _():
                near_copy(chunk, 2).start()

    def ex_copy(g):
        return pltpu.make_async_remote_copy(
            src_ref=ex_tx.at[g], dst_ref=ex_rx.at[g], send_sem=ex_send.at[g], recv_sem=ex_recv.at[g],
            device_id=(1 - pipe, me), device_id_type=MESH,
        )

    def gx_copy(g, which):
        return pltpu.make_async_remote_copy(
            src_ref=txx.at[g, which], dst_ref=rxx.at[g, which],
            send_sem=gx_send.at[g, which], recv_sem=gx_recv.at[g, which],
            device_id=(pipe, partner), device_id_type=MESH,
        )

    def g2_copy(g, which):
        return pltpu.make_async_remote_copy(
            src_ref=tx2.at[g, which], dst_ref=rx2.at[g, which],
            send_sem=g2_send.at[g, which], recv_sem=g2_recv.at[g, which],
            device_id=(pipe, me - 2), device_id_type=MESH,
        )

    def qg_copy(g):
        return pltpu.make_async_copy(
            qgrad.at[g], qg_out.at[0, :, pl.ds(pl.multiple_of(g * WIDE, WIDE), WIDE)], qg_sem.at[g]
        )

    def loss_copy(number, index):
        flip, mask = partners[number][index]
        mine = member(number)
        return pltpu.make_async_remote_copy(
            src_ref=loss_buf.at[number, mine],
            dst_ref=loss_buf.at[number, mine],
            send_sem=loss_send.at[number, index],
            recv_sem=loss_recv.at[number, index],
            device_id=other(flip, mask),
            device_id_type=MESH,
        )

    def loss_start(number, value):
        loss_buf[number, member(number)] = value
        for index in range(len(partners[number])):
            loss_copy(number, index).start()

    def loss_finish(number):
        for index in range(len(partners[number])):
            loss_copy(number, index).wait()
        total = loss_buf[number, 0]
        for place in range(1, len(partners[number]) + 1):
            total = total + loss_buf[number, place]
        return total

    pipe_f = pipe.astype(F32)
    odd_f = odd.astype(F32)

    def query_pair(model, g, hp):
        first = qbuf[model, g, :, pl.ds(hp * PAIR, HEAD_DIM)]
        second = qbuf[model, g, :, pl.ds(hp * PAIR + HEAD_DIM, HEAD_DIM)]
        return jnp.concatenate([first, second], axis=0)

    def wide_iota(axis):
        return lax.broadcasted_iota(jnp.int32, (rows, PAIR), axis)

    def forward(g):
        for model in (STUDENT, TEACHER):
            chunk = 2 * g + model

            @pl.when(has_prev)
            def _():
                far_copy(chunk).wait_recv()

            @pl.when(odd == 1)
            def _():
                near_copy(chunk, 0).start()

        def arrive(model):
            near_copy(2 * g + model, 0).wait_recv()
            pltpu.make_async_copy(
                (tq, sq)[model].at[0, :, pl.ds(0, WIDE)], qbuf.at[model, g], q_sem.at[model, g]
            ).wait()

        arrive(STUDENT)
        slot = lax.rem(g, 2)
        triangle = wide_iota(0) <= lax.rem(wide_iota(1), rows)
        steps = [(model, hp) for model in (STUDENT, TEACHER) for hp in range(PAIRS)]

        def raw_scores(model, hp):
            return dot_nt(win[2 * g + model, 0], query_pair(model, g, hp))

        def finish(model, hp, mixed, inverse):
            cols = pl.ds(hp * PAIR, PAIR)
            mixed = (mixed * inverse).astype(BF16)
            outs[model, g, :, cols] = mixed
            if model == TEACHER:
                student = outs[STUDENT, g, :, cols].astype(F32)
                ex_tx[g, :, cols] = (student - (1.0 + pipe_f) * mixed.astype(F32)).astype(BF16)

        later = raw_scores(*steps[0])
        pending = None
        for index, (model, hp) in enumerate(steps):
            cols = pl.ds(hp * PAIR, PAIR)
            raw = later
            if index + 1 < len(steps):
                if steps[index + 1][0] != model:
                    arrive(steps[index + 1][0])
                later = raw_scores(*steps[index + 1])
            fill = bias[pl.ds(0, rows), :]
            middle = raw[rows : 2 * rows] + jnp.concatenate([fill, fill], axis=1)
            fill = bias[pl.ds(rows, rows), :]
            edge = jnp.where(triangle, raw[2 * rows :], raw[:rows]) + jnp.concatenate([fill, fill], axis=1)
            peak = jnp.max(jnp.maximum(middle, edge), axis=0, keepdims=True)
            middle = jnp.exp2((middle - peak) * to_exp2)
            edge = jnp.exp2((edge - peak) * to_exp2)
            inverse = 1.0 / jnp.sum(middle + edge, axis=0, keepdims=True)
            half = jnp.concatenate(
                [
                    jnp.where(triangle, 0.0, edge).astype(BF16),
                    middle.astype(BF16),
                    jnp.where(triangle, edge, 0.0).astype(BF16),
                ],
                axis=0,
            )
            if model == STUDENT:
                weights[slot, :, cols] = half
                rinv[g, :, cols] = inverse
            if pending is not None:
                finish(*pending)
            if hp == 0:
                values_t = win[2 * g + model, 1].T
            pending = (model, hp, dot(values_t, half), inverse)
        finish(*pending)
        ex_copy(g).start()

    def pass_on(g):
        for which in (1, 0):
            gx_copy(g, which).wait_recv()
            tx2[g, which] = (far_grad[g, which] + odd_f * rxx[g, which].astype(F32)).astype(BF16)

            @pl.when(has_prev)
            def _():
                g2_copy(g, which).start()

    def backward(g):
        slot = lax.rem(g, 2)
        chunk = 2 * g + STUDENT
        ex_copy(g).wait_recv()
        squares = jnp.zeros((8, PAIR), F32)
        for hp in range(PAIRS):
            cols = pl.ds(hp * PAIR, PAIR)
            student = outs[STUDENT, g, :, cols].astype(F32)
            teacher = outs[TEACHER, g, :, cols].astype(F32)
            taken = ex_rx[g, :, cols].astype(F32)
            apart = student - teacher
            first = taken - teacher
            second = taken + apart
            both = first * first + second * second
            squares = squares + jnp.sum(both.reshape(HEAD_DIM // 8, 8, PAIR), axis=0)
            grad = ((2.0 - pipe_f) * apart + taken) * rinv[g, :, cols]
            grad = grad.astype(BF16)
            dnorm[:, cols] = grad
            delta[:, cols] = jnp.sum(grad.astype(F32) * student, axis=0, keepdims=True)
        loss_acc[...] += pipe_f * (squares[:, :HEAD_DIM] + squares[:, HEAD_DIM:])

        @pl.when(g == KV_HEADS - 1)
        def _():
            loss_start(0, loss_acc[...])

        def dprob_of(hp):
            return dot(win[chunk, 1], dnorm[:, pl.ds(hp * PAIR, PAIR)])

        def split(which, grads):
            txx[g, which] = grads[rows : 2 * rows].astype(BF16)
            gx_copy(g, which).start()
            far_grad[g, which] = grads[:rows]
            own_grad[g, which] = grads[2 * rows :]

        later = dprob_of(0)
        split(1, dot_nt(weights[slot], dnorm[...]))

        for hp in range(PAIRS):
            cols = pl.ds(hp * PAIR, PAIR)
            dprob = later
            if hp + 1 < PAIRS:
                later = dprob_of(hp + 1)
            dscore[:, cols] = (weights[slot, :, cols].astype(F32) * (dprob - delta[:, cols])).astype(BF16)
        queries = jnp.concatenate(
            [qbuf[STUDENT, g, :, pl.ds(h * HEAD_DIM, HEAD_DIM)] for h in range(GROUP)], axis=0
        )
        split(0, dot(dscore[...], queries) * scale)
        keys_t = win[chunk, 0].T
        for hp in range(PAIRS):
            query_t = dot(keys_t, dscore[:, pl.ds(hp * PAIR, PAIR)]) * scale
            qgrad[g, :, pl.ds(hp * PAIR, HEAD_DIM)] = query_t[:, :HEAD_DIM].T
            qgrad[g, :, pl.ds(hp * PAIR + HEAD_DIM, HEAD_DIM)] = query_t[:, HEAD_DIM:].T
        qg_copy(g).start()

    def step(g, carry):
        @pl.when(g < KV_HEADS)
        def _():
            forward(g)

        @pl.when(g >= 1)
        def _():
            backward(g - 1)

        @pl.when(g >= 2)
        def _():
            pass_on(g - 2)

        return carry

    lax.fori_loop(0, KV_HEADS + 1, step, 0)
    pass_on(KV_HEADS - 1)

    @pl.when(me >= count - 2)
    def _():
        rx2[...] = jnp.zeros_like(rx2)

    for number in range(1, len(rounds)):
        loss_start(number, loss_finish(number - 1))
    for g in range(KV_HEADS):
        if g == KV_HEADS - 1:
            loss_out[0, 0] = jnp.sum(loss_finish(len(rounds) - 1)) / denominator

        @pl.when(has_next)
        def _():
            g2_copy(g, 0).wait_recv()
            g2_copy(g, 1).wait_recv()

        cols = pl.ds(g * HEAD_DIM, HEAD_DIM)
        for which, out in enumerate((kg_out, vg_out)):
            out[0, :, cols] = (
                own_grad[g, which] + rx2[g, which].astype(F32) + (1.0 - odd_f) * rxx[g, which].astype(F32)
            )

    for chunk in range(2 * KV_HEADS):
        near_copy(chunk, 0).wait_send()

        @pl.when(has_next)
        def _():
            far_copy(chunk).wait_send()

    for g in range(KV_HEADS):
        ex_copy(g).wait_send()
        gx_copy(g, 0).wait_send()
        gx_copy(g, 1).wait_send()
        qg_copy(g).wait()

        @pl.when(has_prev)
        def _():
            g2_copy(g, 0).wait_send()
            g2_copy(g, 1).wait_send()


def hand_over(qg_in, kg_in, vg_in, qg_out, kg_out, vg_out, qg_held, kg_held, vg_held, sems_in, sems_out):
    part = qg_in.shape[1] // PIECES
    rows_of = [pl.ds(k * part, part) for k in range(PIECES)]
    ways = [(qg_in.at[:, r, :], qg_held.at[:, r, :], qg_out.at[:, r, :]) for r in rows_of]
    ways += [(kg_in, kg_held, kg_out), (vg_in, vg_held, vg_out)]
    loads = [pltpu.make_async_copy(src, held, sems_in.at[k]) for k, (src, held, _) in enumerate(ways)]
    stores = [pltpu.make_async_copy(held, dst, sems_out.at[k]) for k, (_, held, dst) in enumerate(ways)]
    for load in loads:
        load.start()
    for load, store in zip(loads, stores):
        load.wait()
        store.start()
    for store in stores:
        store.wait()


def per_device(count, pipes, t_query, t_key, t_value, s_query, s_key, s_value, segment_ids):
    rows = t_query.shape[1]
    span = 3 * rows
    width = KV_HEADS * HEAD_DIM
    denominator = float(pipes * count * rows * HEADS * HEAD_DIM)
    rounds = len(loss_rounds(count))
    dma = pltpu.SemaphoreType.DMA
    anywhere = pl.BlockSpec(memory_space=pltpu.HBM)
    vmem = pl.BlockSpec(memory_space=pltpu.VMEM)
    loss, query_grad, key_grad, value_grad = pl.pallas_call(
        functools.partial(kernel, count, rows, denominator),
        out_shape=(
            jax.ShapeDtypeStruct((1, 1), F32),
            jax.ShapeDtypeStruct((1, rows, HEADS * HEAD_DIM), F32),
            jax.ShapeDtypeStruct((1, rows, width), F32),
            jax.ShapeDtypeStruct((1, rows, width), F32),
        ),
        in_specs=[anywhere] * 6 + [vmem],
        out_specs=(pl.BlockSpec(memory_space=pltpu.SMEM), anywhere, vmem, vmem),
        scratch_shapes=[
            pltpu.VMEM((2 * KV_HEADS, 2, span, HEAD_DIM), BF16),
            pltpu.VMEM((2, KV_HEADS, rows, WIDE), BF16),
            pltpu.VMEM((2 * rows, rows), F32),
            pltpu.VMEM((2, span, WIDE), BF16),
            pltpu.VMEM((2, KV_HEADS, HEAD_DIM, WIDE), BF16),
            pltpu.VMEM((KV_HEADS, 1, WIDE), F32),
            pltpu.VMEM((HEAD_DIM, WIDE), BF16),
            pltpu.VMEM((1, WIDE), F32),
            pltpu.VMEM((span, WIDE), BF16),
            pltpu.VMEM((KV_HEADS, HEAD_DIM, WIDE), BF16),
            pltpu.VMEM((KV_HEADS, HEAD_DIM, WIDE), BF16),
            pltpu.VMEM((KV_HEADS, rows, WIDE), F32),
            pltpu.VMEM((KV_HEADS, 2, rows, HEAD_DIM), F32),
            pltpu.VMEM((KV_HEADS, 2, rows, HEAD_DIM), F32),
            pltpu.VMEM((KV_HEADS, 2, rows, HEAD_DIM), BF16),
            pltpu.VMEM((KV_HEADS, 2, rows, HEAD_DIM), BF16),
            pltpu.VMEM((KV_HEADS, 2, rows, HEAD_DIM), BF16),
            pltpu.VMEM((KV_HEADS, 2, rows, HEAD_DIM), BF16),
            pltpu.VMEM((8, HEAD_DIM), F32),
            pltpu.VMEM((rounds, 8, 8, HEAD_DIM), F32),
            dma((2 * KV_HEADS, 2)),
            dma((2, KV_HEADS)),
            dma((KV_HEADS,)),
            dma((2 * KV_HEADS,)),
            dma((2 * KV_HEADS,)),
            dma((2 * KV_HEADS,)),
            dma((2 * KV_HEADS,)),
            dma((KV_HEADS,)),
            dma((KV_HEADS,)),
            dma((KV_HEADS, 2)),
            dma((KV_HEADS, 2)),
            dma((KV_HEADS, 2)),
            dma((KV_HEADS, 2)),
            dma((rounds, 8)),
            dma((rounds, 8)),
        ],
        compiler_params=pltpu.CompilerParams(
            collective_id=0, has_side_effects=True, vmem_limit_bytes=60 * 1024 * 1024
        ),
        cost_estimate=pl.CostEstimate(
            flops=8 * 2 * HEADS * rows * span * HEAD_DIM,
            bytes_accessed=6 * 1024 * 1024,
            transcendentals=2 * HEADS * rows * span,
        ),
    )(t_query, t_key, t_value, s_query, s_key, s_value, segment_ids.reshape(count, rows))
    grads = (query_grad, key_grad, value_grad)
    query_grad, key_grad, value_grad = pl.pallas_call(
        hand_over,
        out_shape=tuple(jax.ShapeDtypeStruct(grad.shape, F32) for grad in grads),
        in_specs=[pl.BlockSpec(memory_space=pl.ANY)] * 3,
        out_specs=(anywhere,) * 3,
        scratch_shapes=[pltpu.VMEM(grad.shape, F32) for grad in grads] + [dma((PIECES + 2,))] * 2,
        compiler_params=pltpu.CompilerParams(vmem_limit_bytes=63 * 1024 * 1024),
    )(*grads)
    return loss.reshape(()), query_grad, key_grad, value_grad


def solution(mesh):
    spread = P("pipe", "ctx", None)
    return jax.shard_map(
        functools.partial(per_device, mesh.shape["ctx"], mesh.shape["pipe"]),
        mesh=mesh,
        in_specs=(spread,) * 6 + (P(),),
        out_specs=(P(), spread, spread, spread),
        check_vma=False,
    )
```
